32 devices in a mesh: groups: 2 (over y), depth: 4 (over x, core), screen: 4 (over z).
Axes of the slice: x: 2, y: 2, z: 4, core: 2. Of those that a mesh axis runs over, the one named last changes fastest.
Arguments:
- density: float32 [128, 128, 512], P('groups', 'screen', 'depth'), parts along dimension 0, may hold values from 0.05 to 4
- emission: float32 [128, 128, 512], P('groups', 'screen', 'depth'), parts along dimension 0, may hold values from 0.2 to 2
- taps: float32 [8, 512], P('groups', 'depth'), parts along dimension 0, may hold values from 0.05 to 0.5
- shift: int32 [1024], P(('groups', 'depth')), parts along dimension 0, may hold values from -6 to 6
- row_taps: float32 [8, 512], P('groups', 'depth'), parts along dimension 0, may hold values from 0.05 to 0.5
- row_shift: int32 [1024], P(('groups', 'depth')), parts along dimension 0, may hold values from -6 to 6
- step_length: float32 [1024], P(('groups', 'depth')), parts along dimension 0, may hold values from 0.5 to 4
- cotangent: float32 [128, 128], P('groups', 'screen'), parts along dimension 0, may hold values from -1536 to 1536
Outputs:
- grad_density: float32 [128, 128, 512], P('groups', 'screen', 'depth'), parts along dimension 0
- grad_emission: float32 [128, 128, 512], P('groups', 'screen', 'depth'), parts along dimension 0
The draws below stay inside these ranges and needn't reach their ends.
There are 2 independent parts, one for each index of `groups`. The reference program is written for one: setup_inputs(seed, part) draws one part's arguments, and reference() takes and returns one part's arrays. A program takes and returns all parts, laid end to end along the dimension named above; each array names one. Nothing has to cross between parts.
All inputs are finite; a program needn't handle non-finite values.
Results may differ from the reference program's by a relative error of at most 0.000092.
Values sent between devices are 32-bit elements; how exact they have to be, the bound alone decides.
No kernel may reach another device: no remote copies, remote signals or barrier semaphores. Data moves between devices by JAX's collectives and lax.ppermute only.
A program may use at most 64 MiB of HBM per device.

```python
import math
import jax
import jax.numpy as jnp
from jax import lax

ROWS = 64
TAPS = 4
SHIFT = 6
HALO = 8
NX = 128
NZ = 512


def set_ends(entries, rng, smallest, largest):
    extent = entries.shape
    spot = [jax.random.randint(jax.random.fold_in(rng, axis), (), 0, extent[axis]) for axis in range(len(extent))]
    entries = entries.at[tuple(spot)].set(smallest)
    longest = extent.index(max(extent))
    spot[longest] = (spot[longest] + 1) % extent[longest]
    return entries.at[tuple(spot)].set(largest)


def block_levels(rng, dims, pieces, low, high):
    def one(axis_at, shards_of):
        draws = jax.random.uniform(jax.random.fold_in(jax.random.fold_in(rng, 6), axis_at), (shards_of,), jnp.float32, low / len(pieces), high / len(pieces))
        return jnp.repeat(jnp.exp(draws), dims[axis_at] // shards_of).reshape((-1,) + (1,) * (len(dims) - axis_at - 1))

    level = one(*pieces[0])
    for cut in pieces[1:]:
        level = level * one(*cut)
    return level


def bell_draw(stream_key, shape, spread, bound, shards=(), held_as=jnp.bfloat16):
    level = block_levels(stream_key, shape, shards, -0.22, 0.18) if shards else 1.0
    values = jax.random.normal(stream_key, shape, jnp.float32) * spread * level
    return jnp.minimum(jnp.maximum(values, -bound), bound).astype(held_as)


def setup_inputs(seed: int = 0, part: int = 0) -> dict:
    streams_of = jax.random.split(jax.random.key(seed), 9)
    own_keys = jax.random.split(jax.random.fold_in(streams_of[8], part), 9)
    return {
        "density": jnp.clip(jnp.exp(math.log(4.0) - 4.3820266 * jax.random.uniform(own_keys[0], (ROWS, NX, NZ), jnp.float32) ** block_levels(own_keys[0], (ROWS, NX, NZ), ((1, 4), (2, 4)), -0.2, 0.2)), 0.05, 4.0),
        "emission": jnp.clip(0.2 + 1.8 * jax.random.uniform(own_keys[1], (ROWS, NX, NZ), jnp.float32) ** block_levels(own_keys[1], (ROWS, NX, NZ), ((1, 4), (2, 4)), -0.2, 0.2), 0.2, 2.0),
        "taps": jnp.clip(0.05 + 0.45 * jax.random.uniform(own_keys[2], (TAPS, NZ), jnp.float32) ** block_levels(own_keys[2], (TAPS, NZ), ((1, 4),), -0.2, 0.2), 0.05, 0.5),
        "shift": set_ends(jax.random.randint(own_keys[3], (NZ,), -SHIFT, SHIFT + 1), jax.random.fold_in(own_keys[3], 1), -SHIFT, SHIFT).astype(jnp.int32),
        "row_taps": jnp.clip(0.05 + 0.45 * jax.random.uniform(own_keys[4], (TAPS, NZ), jnp.float32) ** block_levels(own_keys[4], (TAPS, NZ), ((1, 4),), -0.2, 0.2), 0.05, 0.5),
        "row_shift": set_ends(jax.random.randint(own_keys[5], (NZ,), -SHIFT, SHIFT + 1), jax.random.fold_in(own_keys[5], 1), -SHIFT, SHIFT).astype(jnp.int32),
        "step_length": jnp.clip(jnp.exp(math.log(4.0) - 2.0794415 * jax.random.uniform(own_keys[6], (NZ,), jnp.float32) ** block_levels(own_keys[6], (NZ,), ((0, 4),), -0.2, 0.2)), 0.5, 4.0),
        "cotangent": bell_draw(own_keys[7], (ROWS, NX), (NZ // 2), 1536.0, ((1, 4),), jnp.float32),
    }


def coefficients(taps, shift):
    offsets = jnp.arange(2 * HALO + 1, dtype=jnp.int32)
    which_tap = jnp.arange(TAPS, dtype=jnp.int32)
    placed = shift[None, None, :] + which_tap[:, None, None] - 1 + HALO
    matches = (placed == offsets[None, :, None]).astype(taps.dtype)
    return jnp.sum(matches * taps[:, None, :], axis=0)


def shifted_sum(field, coefficient, axis, flipped):
    length = field.shape[axis]
    widths = [(0, 0)] * field.ndim
    widths[axis] = (HALO, HALO)
    padded = jnp.pad(field, widths)
    total = jnp.zeros(field.shape, field.dtype)
    for offset in range(2 * HALO + 1):
        begin = 2 * HALO - offset if flipped else offset
        piece = lax.slice_in_dim(padded, begin, begin + length, axis=axis)
        total = total + coefficient[offset] * piece
    return total


def reference(density, emission, taps, shift, row_taps, row_shift, step_length, cotangent):
    coefficient = coefficients(taps, shift)
    row_coefficient = coefficients(row_taps, row_shift)
    sampled_density = shifted_sum(shifted_sum(density, coefficient, 1, False), row_coefficient, 0, False)
    sampled_emission = shifted_sum(shifted_sum(emission, coefficient, 1, False), row_coefficient, 0, False)

    def one_row(items):
        sd_row, se_row, cotangent_row = items
        optical = step_length[None, :] * sd_row / NZ
        running = jnp.cumsum(optical, axis=1)
        before = jnp.concatenate([jnp.zeros_like(optical[:, :1]), running[:, :-1]], axis=1)
        transmit = jnp.exp(-before)
        alpha = -jnp.expm1(-optical)
        light = transmit * alpha * se_row
        reverse_sum = jnp.flip(jnp.cumsum(jnp.flip(light, axis=1), axis=1), axis=1)
        behind = reverse_sum - light
        weight = cotangent_row[:, None]
        grad_optical = weight * (transmit * jnp.exp(-optical) * se_row - behind)
        grad_sd = step_length[None, :] * grad_optical / NZ
        grad_se = weight * transmit * alpha
        return (grad_sd, grad_se)

    grad_sd, grad_se = lax.map(one_row, (sampled_density, sampled_emission, cotangent))
    grad_density = shifted_sum(shifted_sum(grad_sd, row_coefficient, 0, True), coefficient, 1, True)
    grad_emission = shifted_sum(shifted_sum(grad_se, row_coefficient, 0, True), coefficient, 1, True)
    return (grad_density, grad_emission)
```

```python
import functools

import jax
import jax.numpy as jnp
from jax import lax
from jax.experimental import pallas as pl
from jax.experimental.pallas import tpu as pltpu
from jax.sharding import PartitionSpec as P

HALO = 8
REACH = 6
SUB = 8
F32 = jnp.float32
BF16 = jnp.bfloat16
VMEM_LIMIT = 48 * 1024 * 1024


def bits_of(shift):
    moved = jnp.broadcast_to(shift, (SUB, shift.shape[-1])) + REACH
    return {b: (moved & b) != 0 for b in (8, 4, 2, 1)}


def rows_of(taps):
    return [jnp.broadcast_to(taps[k : k + 1, :], (SUB, taps.shape[-1])) for k in range(4)]


def choose(mask, yes, no):
    if yes is None and no is None:
        return None
    if yes is None:
        return jnp.where(mask, 0.0, no)
    if no is None:
        return jnp.where(mask, yes, 0.0)
    return jnp.where(mask, yes, no)


def resample(get, bits, taps, count, flipped):
    way = -1 if flipped else 1
    memo = {}

    def stage(b, i):
        if b == 16:
            key = (b, i)
            if key not in memo:
                memo[key] = get(i)
            return memo[key]
        key = (b, i)
        if key not in memo:
            memo[key] = choose(bits[b], stage(2 * b, i + way * b), stage(2 * b, i))
        return memo[key]

    for i in range(count):
        total = None
        for k in range(4):
            v = stage(1, i + 7 - k if flipped else i - 7 + k)
            if v is not None:
                total = taps[k] * v if total is None else total + taps[k] * v
        yield i, total


def halves(x):
    hi = x.astype(BF16)
    lo = (x - hi.astype(F32)).astype(BF16)
    return jnp.concatenate([hi, lo], axis=1)


def scan_matrix(planes, before):
    a = lax.broadcasted_iota(jnp.int32, (2 * planes, 2 * planes), 0)
    b = lax.broadcasted_iota(jnp.int32, (2 * planes, 2 * planes), 1)
    a = jnp.where(a >= planes, a - planes, a)
    ordered = (a < b) if before else (a > b)
    return jnp.where((b >= planes) | ordered, 1.0, 0.0).astype(BF16)


def edge_kernel(odd_ref, d_ref, e_ref, da, db, ea, eb, sems):
    columns = d_ref.shape[1]
    odd = odd_ref[0]
    first = pl.multiple_of(jnp.where(odd == 1, 0, columns - HALO), HALO)
    second = pl.multiple_of(jnp.where(odd == 1, columns - HALO, 0), HALO)
    copies = [
        pltpu.make_async_copy(ref.at[:, pl.ds(at, HALO), :], out, sems.at[n])
        for n, (ref, at, out) in enumerate(
            ((d_ref, first, da), (d_ref, second, db), (e_ref, first, ea), (e_ref, second, eb))
        )
    ]
    for c in copies:
        c.start()
    for c in copies:
        c.wait()


def row_kernel(d_ref, e_ref, taps_ref, shift_ref, rd_ref, re_ref):
    rows, columns, planes = d_ref.shape
    bits = bits_of(shift_ref[...])
    taps = rows_of(taps_ref[...])

    def body(t, carry):
        at = pl.multiple_of(t * SUB, SUB)
        for ref, out in ((d_ref, rd_ref), (e_ref, re_ref)):
            get = lambda y: ref[y, pl.ds(at, SUB), :] if 0 <= y < rows else None
            for y, v in resample(get, bits, taps, rows, False):
                out[pl.ds(pl.multiple_of(y * columns + at, SUB), SUB), :] = v
        return carry

    lax.fori_loop(0, columns // SUB, body, 0)


def row_halo(odd, a_ref, b_ref, halo_ref, bits, taps):
    rows = a_ref.shape[0]
    for side in range(2):
        use_a = odd == (1 - side)
        get = lambda y: jnp.where(use_a, a_ref[y], b_ref[y]) if 0 <= y < rows else None
        for y, v in resample(get, bits, taps, rows, False):
            halo_ref[pl.ds(y * 2 * HALO + side * HALO, SUB), :] = v


def column_get(r_ref, halo_ref, y0, columns):
    def get(x):
        if x < -HALO or x >= columns + HALO:
            return None
        if x < 0:
            return halo_ref[pl.ds(y0 * 2 * HALO + x + HALO, SUB, stride=2 * HALO), :]
        if x >= columns:
            return halo_ref[pl.ds(y0 * 2 * HALO + HALO + x - columns, SUB, stride=2 * HALO), :]
        return r_ref[pl.ds(y0 * columns + x, SUB, stride=columns), :]

    return get


def pack_totals(totals, dense_ref, group, columns):
    lane = lax.broadcasted_iota(jnp.int32, (SUB, 128), 1)
    per = 128 // columns
    packed = jnp.zeros((SUB, 128), F32)
    base = (group % per) * columns
    for x in range(columns):
        packed = jnp.where(lane == base + x, totals[x * SUB : (x + 1) * SUB, :], packed)
    dense_ref[group // per] += packed


def edges_out(odd, ref, a_ref, b_ref):
    columns = ref.shape[0]
    first = jnp.where(odd == 1, 0, columns - HALO)
    second = jnp.where(odd == 1, columns - HALO, 0)
    a_ref[...] = ref[pl.ds(first, HALO)]
    b_ref[...] = ref[pl.ds(second, HALO)]


def density_kernel(
    odd_ref, rd_ref, a_ref, b_ref, row_taps_ref, row_shift_ref, taps_ref, shift_ref, scale_ref,
    q_ref, n_ref, qa_ref, qb_ref, dense_ref, halo_ref,
):
    odd = odd_ref[0]
    columns, rows, planes = q_ref.shape
    row_halo(odd, a_ref, b_ref, halo_ref, bits_of(row_shift_ref[...]), rows_of(row_taps_ref[...]))
    bits = bits_of(shift_ref[...])
    taps = rows_of(taps_ref[...])
    scale = jnp.broadcast_to(scale_ref[...], (SUB, planes))
    matrix = scan_matrix(planes, True)
    dense_ref[...] = jnp.zeros_like(dense_ref)

    def body(group, carry):
        y0 = group * SUB
        get = column_get(rd_ref, halo_ref, y0, columns)
        pieces = [scale * v for _, v in resample(get, bits, taps, columns, False)]
        optical = jnp.concatenate(pieces, axis=0)
        sums = jnp.dot(halves(optical), matrix, preferred_element_type=F32)
        transmit = jnp.exp(-sums[:, :planes])
        series = optical * (1.0 - optical * (1 / 2) * (1.0 - optical * (1 / 3) * (1.0 - optical * (1 / 4) * (
            1.0 - optical * (1 / 5) * (1.0 - optical * (1 / 6))))))
        alpha = jnp.where(optical < 0.25, series, 1.0 - jnp.exp(-optical))
        q = transmit * alpha
        n = transmit - q
        at = pl.multiple_of(y0, SUB)
        for x in range(columns):
            q_ref[x, pl.ds(at, SUB), :] = q[x * SUB : (x + 1) * SUB]
            n_ref[x, pl.ds(at, SUB), :] = n[x * SUB : (x + 1) * SUB]
        pack_totals(sums[:, planes:], dense_ref, group, columns)
        return carry

    lax.fori_loop(0, rows // SUB, body, 0)
    edges_out(odd, q_ref, qa_ref, qb_ref)


def emission_kernel(
    odd_ref, re_ref, a_ref, b_ref, q_ref, n_ref, row_taps_ref, row_shift_ref, taps_ref, shift_ref, scale_ref,
    p_ref, pa_ref, pb_ref, dense_ref, halo_ref,
):
    odd = odd_ref[0]
    columns, rows, planes = p_ref.shape
    row_halo(odd, a_ref, b_ref, halo_ref, bits_of(row_shift_ref[...]), rows_of(row_taps_ref[...]))
    bits = bits_of(shift_ref[...])
    taps = rows_of(taps_ref[...])
    scale = jnp.broadcast_to(scale_ref[...], (SUB, planes))
    matrix = scan_matrix(planes, False)
    dense_ref[...] = jnp.zeros_like(dense_ref)

    def body(group, carry):
        y0 = group * SUB
        at = pl.multiple_of(y0, SUB)
        get = column_get(re_ref, halo_ref, y0, columns)
        pieces = [v for _, v in resample(get, bits, taps, columns, False)]
        light = jnp.concatenate([q_ref[x, pl.ds(at, SUB), :] * pieces[x] for x in range(columns)], axis=0)
        sums = jnp.dot(halves(light), matrix, preferred_element_type=F32)
        for x in range(columns):
            behind = sums[x * SUB : (x + 1) * SUB, :planes]
            p_ref[x, pl.ds(at, SUB), :] = scale * (n_ref[x, pl.ds(at, SUB), :] * pieces[x] - behind)
        pack_totals(sums[:, planes:], dense_ref, group, columns)
        return carry

    lax.fori_loop(0, rows // SUB, body, 0)
    edges_out(odd, p_ref, pa_ref, pb_ref)


def join_kernel(count, mine_ref, weight_ref, *refs):
    out_ref = refs[-1]
    mine = mine_ref[0]
    weight = weight_ref[...]
    own = refs[0]
    front = jnp.zeros_like(weight)
    for ahead in range(1, count):
        front += jnp.where(mine + ahead >= count, refs[ahead][0], 0.0)
    running = front + own[0]
    back = jnp.zeros_like(weight)
    for ahead in range(1, count):
        there = mine + ahead < count
        back += jnp.where(there, jnp.exp(-running) * refs[ahead][1], 0.0)
        running += jnp.where(there, refs[ahead][0], 0.0)
    out_ref[0] = weight * jnp.exp(-front)
    out_ref[1] = weight * back


def spread(dense, base, columns, first, last):
    lane = lax.broadcasted_iota(jnp.int32, (SUB, 128), 1)
    wanted = jnp.concatenate(
        [jnp.where(lane == base + x, dense, 0.0) for x in range(first, last)], axis=0
    )
    ones = jnp.ones((256, 128), BF16)
    return jnp.dot(halves(wanted), ones, preferred_element_type=F32)


def final_kernel(
    odd_ref, p_ref, q_ref, pa_ref, pb_ref, qa_ref, qb_ref, own_ref, wa_ref, wb_ref,
    row_taps_ref, row_shift_ref, taps_ref, shift_ref, scale_ref,
    gd_ref, ge_ref, cd_ref, ce_ref,
):
    odd = odd_ref[0]
    columns, rows, planes = p_ref.shape
    per = 128 // columns
    bits = bits_of(shift_ref[...])
    taps = rows_of(taps_ref[...])
    scale = jnp.broadcast_to(scale_ref[...], (SUB, planes))

    def body(group, carry):
        y0 = group * SUB
        at = pl.multiple_of(y0, SUB)
        chunk = group // per
        base = (group % per) * columns
        left_a = odd == 1
        left_w = [jnp.where(left_a, wa_ref[f, chunk], wb_ref[f, chunk]) for f in range(2)]
        right_w = [jnp.where(left_a, wb_ref[f, chunk], wa_ref[f, chunk]) for f in range(2)]
        own = [spread(own_ref[f, chunk], base, columns, 0, columns) for f in range(2)]
        left = [spread(left_w[f], base, columns, columns - HALO, columns) for f in range(2)]
        right = [spread(right_w[f], base, columns, 0, HALO) for f in range(2)]

        def weights(x):
            if x < 0:
                return [w[(x + HALO) * SUB : (x + HALO + 1) * SUB] for w in left]
            if x >= columns:
                return [w[(x - columns) * SUB : (x - columns + 1) * SUB] for w in right]
            return [w[x * SUB : (x + 1) * SUB] for w in own]

        def local(ref, ra, rb, x):
            if x < 0:
                return jnp.where(left_a, ra[x + HALO, pl.ds(at, SUB), :], rb[x + HALO, pl.ds(at, SUB), :])
            if x >= columns:
                return jnp.where(left_a, rb[x - columns, pl.ds(at, SUB), :], ra[x - columns, pl.ds(at, SUB), :])
            return ref[x, pl.ds(at, SUB), :]

        def get_d(x):
            if x < -HALO or x >= columns + HALO:
                return None
            f, b = weights(x)
            return f * local(p_ref, pa_ref, pb_ref, x) - b * scale

        def get_e(x):
            if x < -HALO or x >= columns + HALO:
                return None
            return weights(x)[0] * local(q_ref, qa_ref, qb_ref, x)

        for get, out in ((get_d, cd_ref), (get_e, ce_ref)):
            for x, v in resample(get, bits, taps, columns, True):
                out[pl.ds(y0 * columns + x, SUB, stride=columns), :] = v
        return carry

    lax.fori_loop(0, rows // SUB, body, 0)
    row_bits = bits_of(row_shift_ref[...])
    row_taps = rows_of(row_taps_ref[...])

    def row_body(t, carry):
        at = pl.multiple_of(t * SUB, SUB)
        for ref, out in ((cd_ref, gd_ref), (ce_ref, ge_ref)):
            get = lambda y: ref[pl.ds(pl.multiple_of(y * columns + at, SUB), SUB), :] if 0 <= y < rows else None
            for y, v in resample(get, row_bits, row_taps, rows, True):
                out[y, pl.ds(at, SUB), :] = v
        return carry

    lax.fori_loop(0, columns // SUB, row_body, 0)


def call(kernel, outs, scalars, vmem, scratch=(), anywhere=False, micros=2.0):
    space = pl.ANY if anywhere else pltpu.VMEM
    return pl.pallas_call(
        kernel,
        out_shape=[jax.ShapeDtypeStruct(s, F32) for s in outs],
        in_specs=[pl.BlockSpec(memory_space=pltpu.SMEM)] * len(scalars)
        + [pl.BlockSpec(memory_space=space)] * len(vmem),
        out_specs=[pl.BlockSpec(memory_space=space)] * len(outs),
        scratch_shapes=list(scratch),
        compiler_params=pltpu.CompilerParams(vmem_limit_bytes=VMEM_LIMIT),
        cost_estimate=pl.CostEstimate(
            flops=int(micros * 1e6), bytes_accessed=int(micros * 3.0e6), transcendentals=0
        ),
    )(*scalars, *vmem)


def swap(value, axis, parity):
    count = lax.axis_size(axis)
    pairs = []
    for i in range(parity, count - 1, 2):
        pairs += [(i, i + 1), (i + 1, i)]
    return lax.ppermute(value, axis, pairs)


def on_device(density, emission, taps, shift, row_taps, row_shift, step_length, cotangent):
    rows, columns, planes = density.shape
    slabs = lax.axis_size("depth")
    all_planes = planes * slabs
    per = 128 // columns
    chunks = rows // SUB // per
    shift, row_shift = shift[None, :], row_shift[None, :]
    scale = step_length[None, :] / all_planes
    odd = (lax.axis_index("screen") % 2).astype(jnp.int32)[None]
    mine = lax.axis_index("depth").astype(jnp.int32)[None]
    weight = cotangent.reshape(chunks, per, SUB, columns).transpose(0, 2, 1, 3).reshape(chunks, SUB, 128)

    edge = (rows, HALO, planes)
    da, db, ea, eb = call(
        edge_kernel, [edge] * 4, [odd], [density, emission], [pltpu.SemaphoreType.DMA((4,))], anywhere=True
    )
    da, db = swap(da, "screen", 0), swap(db, "screen", 1)
    ea, eb = swap(ea, "screen", 0), swap(eb, "screen", 1)
    flat = (rows * columns, planes)
    rd, re = call(row_kernel, [flat, flat], [], [density, emission, row_taps, row_shift])

    cells = (columns, rows, planes)
    side = (HALO, rows, planes)
    dense = (chunks, SUB, 128)
    halo = pltpu.VMEM((rows * 2 * HALO, planes), F32)
    q, n, qa, qb, slab_optical = call(
        density_kernel,
        [cells, cells, side, side, dense],
        [odd],
        [rd, da, db, row_taps, row_shift, taps, shift, scale],
        [halo],
    )
    qa, qb = swap(qa, "screen", 0), swap(qb, "screen", 1)
    p, pa, pb, slab_light = call(
        emission_kernel,
        [cells, side, side, dense],
        [odd],
        [re, ea, eb, q, n, row_taps, row_shift, taps, shift, scale],
        [halo],
    )
    pa, pb = swap(pa, "screen", 0), swap(pb, "screen", 1)
    sums = jnp.stack([slab_optical, slab_light])
    ahead = [sums] + [
        lax.ppermute(sums, "depth", [((i + e) % slabs, i) for i in range(slabs)]) for e in range(1, slabs)
    ]
    (own,) = call(
        functools.partial(join_kernel, slabs), [(2,) + dense], [mine], [weight] + ahead, micros=0.3
    )
    wa, wb = swap(own, "screen", 0), swap(own, "screen", 1)
    gd, ge = call(
        final_kernel,
        [density.shape, density.shape],
        [odd],
        [p, q, pa, pb, qa, qb, own, wa, wb, row_taps, row_shift, taps, shift, scale],
        [pltpu.VMEM(flat, F32), pltpu.VMEM(flat, F32)],
        micros=4.0,
    )
    return gd, ge


def solution(mesh):
    in_specs = (
        P("groups", "screen", "depth"),
        P("groups", "screen", "depth"),
        P("groups", "depth"),
        P(("groups", "depth")),
        P("groups", "depth"),
        P(("groups", "depth")),
        P(("groups", "depth")),
        P("groups", "screen"),
    )
    out_specs = (P("groups", "screen", "depth"), P("groups", "screen", "depth"))
    return jax.shard_map(
        on_device, mesh=mesh, in_specs=in_specs, out_specs=out_specs, check_vma=False
    )
```

```python
import functools

import jax
import jax.numpy as jnp
from jax import lax
from jax.experimental import pallas as pl
from jax.experimental.pallas import tpu as pltpu
from jax.sharding import PartitionSpec as P

HALO = 8
REACH = 6
SUB = 8
F32 = jnp.float32
BF16 = jnp.bfloat16
VMEM_LIMIT = 48 * 1024 * 1024
UNROLL = 4


def pitch_of(columns):
    return columns + 1


def loop(count, body):
    def step(i, carry):
        body(i)
        return carry

    lax.fori_loop(0, count, step, 0, unroll=min(count, UNROLL))


def bits_of(shift):
    moved = jnp.broadcast_to(shift, (SUB, shift.shape[-1])) + REACH
    return {b: (moved & b) != 0 for b in (8, 4, 2, 1)}


def rows_of(taps):
    return [jnp.broadcast_to(taps[k : k + 1, :], (SUB, taps.shape[-1])) for k in range(4)]


def choose(mask, yes, no):
    if yes is None and no is None:
        return None
    if yes is None:
        return jnp.where(mask, 0.0, no)
    if no is None:
        return jnp.where(mask, yes, 0.0)
    return jnp.where(mask, yes, no)


def resample(get, bits, taps, count, flipped):
    way = -1 if flipped else 1
    memo = {}

    def stage(b, i):
        if b == 16:
            key = (b, i)
            if key not in memo:
                memo[key] = get(i)
            return memo[key]
        key = (b, i)
        if key not in memo:
            memo[key] = choose(bits[b], stage(2 * b, i + way * b), stage(2 * b, i))
        return memo[key]

    for i in range(count):
        total = None
        for k in range(4):
            v = stage(1, i + 7 - k if flipped else i - 7 + k)
            if v is not None:
                total = taps[k] * v if total is None else total + taps[k] * v
        yield i, total


def halves(x):
    hi = x.astype(BF16)
    lo = (x - hi.astype(F32)).astype(BF16)
    return jnp.concatenate([hi, lo], axis=1)


def scan_matrix(planes, before):
    a = lax.broadcasted_iota(jnp.int32, (2 * planes, 2 * planes), 0)
    b = lax.broadcasted_iota(jnp.int32, (2 * planes, 2 * planes), 1)
    a = jnp.where(a >= planes, a - planes, a)
    ordered = (a < b) if before else (a > b)
    return jnp.where((b >= planes) | ordered, 1.0, 0.0).astype(BF16)


def edge_kernel(odd_ref, field_ref, a_ref, b_ref, sems):
    columns = field_ref.shape[1]
    odd = odd_ref[0]
    first = pl.multiple_of(jnp.where(odd == 1, 0, columns - HALO), HALO)
    second = pl.multiple_of(jnp.where(odd == 1, columns - HALO, 0), HALO)
    copies = [
        pltpu.make_async_copy(field_ref.at[:, pl.ds(at, HALO), :], out, sems.at[n])
        for n, (at, out) in enumerate(((first, a_ref), (second, b_ref)))
    ]
    for c in copies:
        c.start()
    for c in copies:
        c.wait()


def row_kernel(d_ref, e_ref, taps_ref, shift_ref, weight_ref, rd_ref, re_ref):
    rows, columns, planes = d_ref.shape
    bits = bits_of(shift_ref[...])
    taps = rows_of(taps_ref[...])

    pitch = pitch_of(columns)

    def body(t):
        at = pl.multiple_of(t * SUB, SUB)
        for ref, out in ((d_ref, rd_ref), (e_ref, re_ref)):
            get = lambda y: ref[y, pl.ds(at, SUB), :] if 0 <= y < rows else None
            for y, v in resample(get, bits, taps, rows, False):
                out[pl.ds(y * pitch + at, SUB), :] = v

    loop(columns // SUB, body)


def row_halo(odd, a_ref, b_ref, halo_ref, bits, taps):
    rows = a_ref.shape[0]
    for side in range(2):
        use_a = odd == (1 - side)
        get = lambda y: jnp.where(use_a, a_ref[y], b_ref[y]) if 0 <= y < rows else None
        for y, v in resample(get, bits, taps, rows, False):
            halo_ref[pl.ds(y * pitch_of(2 * HALO) + side * HALO, SUB), :] = v


def column_get(r_ref, halo_ref, y0, columns):
    pitch, side_pitch = pitch_of(columns), pitch_of(2 * HALO)

    def get(x):
        if x < -HALO or x >= columns + HALO:
            return None
        if x < 0:
            return halo_ref[pl.ds(y0 * side_pitch + x + HALO, SUB, stride=side_pitch), :]
        if x >= columns:
            return halo_ref[pl.ds(y0 * side_pitch + HALO + x - columns, SUB, stride=side_pitch), :]
        return r_ref[pl.ds(y0 * pitch + x, SUB, stride=pitch), :]

    return get


def pack_totals(totals, dense_ref, group, columns):
    lane = lax.broadcasted_iota(jnp.int32, (SUB, 128), 1)
    per = 128 // columns
    packed = jnp.zeros((SUB, 128), F32)
    base = (group % per) * columns
    for x in range(columns):
        packed = jnp.where(lane == base + x, totals[x * SUB : (x + 1) * SUB, :], packed)
    dense_ref[group // per] += packed


def edges_out(odd, ref, a_ref, b_ref):
    columns = ref.shape[0]
    first = jnp.where(odd == 1, 0, columns - HALO)
    second = jnp.where(odd == 1, columns - HALO, 0)
    a_ref[...] = ref[pl.ds(first, HALO)]
    b_ref[...] = ref[pl.ds(second, HALO)]


def absorbed(optical):
    series = 1.0 - optical * (1 / 6)
    for k in (5, 4, 3, 2):
        series = 1.0 - optical * (1 / k) * series
    return jnp.where(optical < 0.25, optical * series, 1.0 - jnp.exp(-optical))


def density_kernel(
    odd_ref, rd_ref, a_ref, b_ref, row_taps_ref, row_shift_ref, taps_ref, shift_ref, scale_ref,
    q_ref, n_ref, qa_ref, qb_ref, dense_ref, halo_ref, optical_ref, split_ref, sums_ref,
):
    odd = odd_ref[0]
    columns, rows, planes = q_ref.shape
    row_halo(odd, a_ref, b_ref, halo_ref, bits_of(row_shift_ref[...]), rows_of(row_taps_ref[...]))
    bits = bits_of(shift_ref[...])
    taps = rows_of(taps_ref[...])
    scale = jnp.broadcast_to(scale_ref[...], (SUB, planes))
    matrix = scan_matrix(planes, True)
    dense_ref[...] = jnp.zeros_like(dense_ref)

    def body(group):
        y0 = group * SUB
        get = column_get(rd_ref, halo_ref, y0, columns)
        held = []
        for x, v in resample(get, bits, taps, columns, False):
            at = pl.multiple_of((group * columns + x) * SUB, SUB)
            v = scale * v
            optical_ref[pl.ds(at, SUB), :] = v
            held.append(v)
            if x % 2:
                at = pl.multiple_of((group * columns + x - 1) * SUB, 2 * SUB)
                split_ref[pl.ds(at, 2 * SUB), :] = halves(jnp.concatenate(held, axis=0))
                held = []

    loop(rows // SUB, body)
    sums_ref[...] = jnp.dot(split_ref[...], matrix, preferred_element_type=F32)

    def finish(group):
        to = pl.ds(pl.multiple_of(group * SUB, SUB), SUB)
        totals = []
        for x in range(columns):
            at = pl.ds(pl.multiple_of((group * columns + x) * SUB, SUB), SUB)
            optical = optical_ref[at, :]
            transmit = jnp.exp(-sums_ref[at, :planes])
            q = transmit * absorbed(optical)
            q_ref[x, to, :] = q
            n_ref[x, to, :] = transmit - q
            totals.append(sums_ref[at, planes:])
        pack_totals(jnp.concatenate(totals, axis=0), dense_ref, group, columns)

    loop(rows // SUB, finish)
    edges_out(odd, q_ref, qa_ref, qb_ref)


def emission_kernel(
    odd_ref, re_ref, a_ref, b_ref, q_ref, n_ref, row_taps_ref, row_shift_ref, taps_ref, shift_ref, scale_ref,
    p_ref, dense_ref, halo_ref,
):
    odd = odd_ref[0]
    columns, rows, planes = p_ref.shape
    row_halo(odd, a_ref, b_ref, halo_ref, bits_of(row_shift_ref[...]), rows_of(row_taps_ref[...]))
    bits = bits_of(shift_ref[...])
    taps = rows_of(taps_ref[...])
    scale = jnp.broadcast_to(scale_ref[...], (SUB, planes))
    matrix = scan_matrix(planes, False)
    dense_ref[...] = jnp.zeros_like(dense_ref)

    def body(group):
        y0 = group * SUB
        at = pl.multiple_of(y0, SUB)
        get = column_get(re_ref, halo_ref, y0, columns)
        pieces = [v for _, v in resample(get, bits, taps, columns, False)]
        light = jnp.concatenate([q_ref[x, pl.ds(at, SUB), :] * pieces[x] for x in range(columns)], axis=0)
        sums = jnp.dot(halves(light), matrix, preferred_element_type=F32)
        for x in range(columns):
            behind = sums[x * SUB : (x + 1) * SUB, :planes]
            p_ref[x, pl.ds(at, SUB), :] = scale * (n_ref[x, pl.ds(at, SUB), :] * pieces[x] - behind)
        pack_totals(sums[:, planes:], dense_ref, group, columns)

    loop(rows // SUB, body)


def join_kernel(count, odd_ref, mine_ref, weight_ref, p_ref, *refs):
    sums, (out_ref, a_ref, b_ref) = refs[:count], refs[count:]
    mine = mine_ref[0]
    weight = weight_ref[...]
    front = jnp.zeros_like(weight)
    for ahead in range(1, count):
        front += jnp.where(mine + ahead >= count, sums[ahead][0], 0.0)
    running = front + sums[0][0]
    back = jnp.zeros_like(weight)
    for ahead in range(1, count):
        there = mine + ahead < count
        back += jnp.where(there, jnp.exp(-running) * sums[ahead][1], 0.0)
        running += jnp.where(there, sums[ahead][0], 0.0)
    out_ref[0] = weight * jnp.exp(-front)
    out_ref[1] = weight * back
    columns = p_ref.shape[0]
    for ref, at in (
        (a_ref, jnp.where(odd_ref[0] == 1, 0, columns - HALO)),
        (b_ref, jnp.where(odd_ref[0] == 1, columns - HALO, 0)),
    ):
        rows = p_ref.shape[1]
        for x in range(HALO):
            ref[x * rows : (x + 1) * rows, :] = p_ref[at + x]
        for f in range(2):
            for c in range(weight.shape[0]):
                row = HALO * rows + (f * weight.shape[0] + c) * SUB
                ref[row : row + SUB, :] = out_ref[f, c]


def spread(pair, base, first, last):
    lane = lax.broadcasted_iota(jnp.int32, (SUB, 128), 1)
    masks = [lane == base + x for x in range(first, last)]
    rows = []
    for dense in pair:
        hi = dense.astype(BF16).astype(F32)
        stacks = [
            jnp.concatenate([jnp.where(m, part, 0.0) for m in masks], axis=0).astype(BF16)
            for part in (hi, dense - hi)
        ]
        rows.append(jnp.concatenate(stacks, axis=1))
    ones = jnp.ones((256, 128), BF16)
    return [jnp.dot(r, ones, preferred_element_type=F32) for r in rows]


def own_kernel(
    p_ref, q_ref, own_ref, row_taps_ref, row_shift_ref, taps_ref, shift_ref, scale_ref,
    gd_ref, ge_ref, td_ref, te_ref, cd_ref, ce_ref, out_ref, front_ref, back_ref, sems,
):
    columns, rows, planes = p_ref.shape
    per = 128 // columns
    inner = columns - 2 * HALO
    pitch, side_pitch = pitch_of(inner), pitch_of(2 * HALO)
    bits = bits_of(shift_ref[...])
    taps = rows_of(taps_ref[...])
    scale = jnp.broadcast_to(scale_ref[...], (SUB, planes))

    for group in range(rows // SUB):
        chunk = group // per
        front, back = spread((own_ref[0, chunk], own_ref[1, chunk]), group % per * columns, 0, columns)
        for x in range(columns):
            front_ref[x, group * SUB : (group + 1) * SUB, :] = front[x * SUB : (x + 1) * SUB]
            back_ref[x, group * SUB : (group + 1) * SUB, :] = back[x * SUB : (x + 1) * SUB] * scale

    def body(group):
        y0 = group * SUB
        at = pl.multiple_of(y0, SUB)

        def get_d(x):
            if not 0 <= x < columns:
                return None
            return front_ref[x, pl.ds(at, SUB), :] * p_ref[x, pl.ds(at, SUB), :] - back_ref[x, pl.ds(at, SUB), :]

        def get_e(x):
            if not 0 <= x < columns:
                return None
            return front_ref[x, pl.ds(at, SUB), :] * q_ref[x, pl.ds(at, SUB), :]

        for get, inside, outside in ((get_d, cd_ref, td_ref), (get_e, ce_ref, te_ref)):
            for x, v in resample(get, bits, taps, columns, True):
                if HALO <= x < columns - HALO:
                    inside[pl.ds(y0 * pitch + x - HALO, SUB, stride=pitch), :] = v
                else:
                    to = x if x < HALO else x - inner
                    outside[pl.ds(y0 * side_pitch + to, SUB, stride=side_pitch), :] = v

    loop(rows // SUB, body)
    row_bits = bits_of(row_shift_ref[...])
    row_taps = rows_of(row_taps_ref[...])
    copies = []
    for field, (ref, out) in enumerate(((cd_ref, gd_ref), (ce_ref, ge_ref))):
        def row_body(t):
            at = pl.multiple_of(t * SUB, SUB)
            get = lambda y: ref[pl.ds(y * pitch + at, SUB), :] if 0 <= y < rows else None
            for y, v in resample(get, row_bits, row_taps, rows, True):
                out_ref[field, y, pl.ds(at, SUB), :] = v

        loop(inner // SUB, row_body)
        copies.append(
            pltpu.make_async_copy(out_ref.at[field], out.at[:, pl.ds(HALO, inner), :], sems.at[field])
        )
        copies[-1].start()
    for c in copies:
        c.wait()


def outer_kernel(
    odd_ref, pa_ref, pb_ref, qa_ref, qb_ref, td_ref, te_ref,
    row_taps_ref, row_shift_ref, taps_ref, shift_ref, scale_ref, gd_in, ge_in,
    gd_ref, ge_ref, cd_ref, ce_ref, out_ref, front_ref, back_ref, sems,
):
    odd = odd_ref[0]
    rows, columns, planes = gd_ref.shape
    per = 128 // columns
    chunks = rows // SUB // per
    pitch = pitch_of(2 * HALO)
    bits = bits_of(shift_ref[...])
    taps = rows_of(taps_ref[...])
    scale = jnp.broadcast_to(scale_ref[...], (SUB, planes))
    use_a = (odd == 1, odd != 1)

    for side in range(2):
        first = columns - HALO if side == 0 else 0
        for group in range(rows // SUB):
            pair = []
            for f in range(2):
                row = HALO * rows + (f * chunks + group // per) * SUB
                pair.append(
                    jnp.where(use_a[side], pa_ref[row : row + SUB, :], pb_ref[row : row + SUB, :])
                )
            front, back = spread(pair, group % per * columns, first, first + HALO)
            for x in range(HALO):
                front_ref[side, x, group * SUB : (group + 1) * SUB, :] = front[x * SUB : (x + 1) * SUB]
                back_ref[side, x, group * SUB : (group + 1) * SUB, :] = back[x * SUB : (x + 1) * SUB] * scale

    def body(group):
        y0 = group * SUB
        at = pl.multiple_of(y0, SUB)
        for side in range(2):
            start = -HALO if side == 0 else HALO

            def get_d(x):
                i = x - start
                if not 0 <= i < HALO:
                    return None
                here = pl.ds(pl.multiple_of(i * rows + at, SUB), SUB)
                v = jnp.where(use_a[side], pa_ref[here, :], pb_ref[here, :])
                return front_ref[side, i, pl.ds(at, SUB), :] * v - back_ref[side, i, pl.ds(at, SUB), :]

            def get_e(x):
                i = x - start
                if not 0 <= i < HALO:
                    return None
                v = jnp.where(use_a[side], qa_ref[i, pl.ds(at, SUB), :], qb_ref[i, pl.ds(at, SUB), :])
                return front_ref[side, i, pl.ds(at, SUB), :] * v

            for get, ref, out in ((get_d, td_ref, cd_ref), (get_e, te_ref, ce_ref)):
                for x, v in resample(get, bits, taps, HALO, True):
                    where = pl.ds(y0 * pitch + side * HALO + x, SUB, stride=pitch)
                    out[where, :] = ref[where, :] if v is None else ref[where, :] + v

    loop(rows // SUB, body)
    row_bits = bits_of(row_shift_ref[...])
    row_taps = rows_of(row_taps_ref[...])
    copies = []
    for field, (ref, out) in enumerate(((cd_ref, gd_ref), (ce_ref, ge_ref))):
        for side in range(2):
            get = lambda y: ref[pl.ds(y * pitch + side * HALO, SUB), :] if 0 <= y < rows else None
            for y, v in resample(get, row_bits, row_taps, rows, True):
                out_ref[field, side, y] = v
            copies.append(
                pltpu.make_async_copy(
                    out_ref.at[field, side],
                    out.at[:, pl.ds(side * (columns - HALO), HALO), :],
                    sems.at[2 * field + side],
                )
            )
            copies[-1].start()
    for c in copies:
        c.wait()


def call(kernel, outs, scalars, vmem, scratch=(), hbm_in=(), hbm_out=0, aliases=None, micros=2.0, limit=VMEM_LIMIT):
    whole, far = pl.BlockSpec(memory_space=pltpu.VMEM), pl.BlockSpec(memory_space=pl.ANY)
    return pl.pallas_call(
        kernel,
        out_shape=[jax.ShapeDtypeStruct(s, F32) for s in outs],
        in_specs=[pl.BlockSpec(memory_space=pltpu.SMEM)] * len(scalars)
        + [whole] * len(vmem)
        + [far] * len(hbm_in),
        out_specs=[far] * hbm_out + [whole] * (len(outs) - hbm_out),
        scratch_shapes=list(scratch),
        input_output_aliases=aliases or {},
        compiler_params=pltpu.CompilerParams(vmem_limit_bytes=limit),
        cost_estimate=pl.CostEstimate(
            flops=int(micros * 1e6), bytes_accessed=int(micros * 3.0e6), transcendentals=0
        ),
    )(*scalars, *vmem, *hbm_in)


def swap(value, axis, parity):
    count = lax.axis_size(axis)
    pairs = []
    for i in range(parity, count - 1, 2):
        pairs += [(i, i + 1), (i + 1, i)]
    return lax.ppermute(value, axis, pairs)


def on_device(density, emission, taps, shift, row_taps, row_shift, step_length, cotangent):
    rows, columns, planes = density.shape
    slabs = lax.axis_size("depth")
    all_planes = planes * slabs
    per = 128 // columns
    chunks = rows // SUB // per
    shift, row_shift = shift[None, :], row_shift[None, :]
    scale = step_length[None, :] / all_planes
    odd = (lax.axis_index("screen") % 2).astype(jnp.int32)[None]
    mine = lax.axis_index("depth").astype(jnp.int32)[None]
    weight = cotangent.reshape(chunks, per, SUB, columns).transpose(0, 2, 1, 3).reshape(chunks, SUB, 128)

    edge = (rows, HALO, planes)
    sides = []
    for field in (density, emission):
        a, b = call(
            edge_kernel,
            [edge] * 2,
            [odd],
            [],
            [pltpu.SemaphoreType.DMA((2,))],
            hbm_in=[field],
            hbm_out=2,
            micros=0.2,
        )
        sides.append((swap(a, "screen", 0), swap(b, "screen", 1)))
    (da, db), (ea, eb) = sides
    flat = (rows * pitch_of(columns), planes)
    rd, re = call(row_kernel, [flat, flat], [], [density, emission, row_taps, row_shift, weight])

    cells = (columns, rows, planes)
    side = (HALO, rows, planes)
    dense = (chunks, SUB, 128)
    outer = (rows * pitch_of(2 * HALO), planes)
    q, n, qa, qb, slab_optical = call(
        density_kernel,
        [cells, cells, side, side, dense],
        [odd],
        [rd, da, db, row_taps, row_shift, taps, shift, scale],
        [
            pltpu.VMEM(outer, F32),
            pltpu.VMEM((rows * columns, planes), F32),
            pltpu.VMEM((rows * columns, 2 * planes), BF16),
            pltpu.VMEM((rows * columns, 2 * planes), F32),
        ],
    )
    qa, qb = swap(qa, "screen", 0), swap(qb, "screen", 1)
    p, slab_light = call(
        emission_kernel,
        [cells, dense],
        [odd],
        [re, ea, eb, q, n, row_taps, row_shift, taps, shift, scale],
        [pltpu.VMEM(outer, F32)],
        micros=6.0,
    )
    sums = jnp.stack([slab_optical, slab_light])
    ahead = [sums] + [
        lax.ppermute(sums, "depth", [((i + e) % slabs, i) for i in range(slabs)]) for e in range(1, slabs)
    ]
    message = (HALO * rows + 2 * chunks * SUB, planes)
    own, pa, pb = call(
        functools.partial(join_kernel, slabs),
        [(2,) + dense, message, message],
        [odd, mine],
        [weight, p] + ahead,
        micros=0.3,
    )
    pa, pb, qa, qb = lax.optimization_barrier((pa, pb, qa, qb))
    pa, pb = swap(pa, "screen", 0), swap(pb, "screen", 1)
    inner = (rows * pitch_of(columns - 2 * HALO), planes)
    gd, ge, td, te = call(
        own_kernel,
        [density.shape, density.shape, outer, outer],
        [],
        [p, q, own, row_taps, row_shift, taps, shift, scale],
        [
            pltpu.VMEM(inner, F32),
            pltpu.VMEM(inner, F32),
            pltpu.VMEM((2, rows, columns - 2 * HALO, planes), F32),
            pltpu.VMEM(cells, F32),
            pltpu.VMEM(cells, F32),
            pltpu.SemaphoreType.DMA((2,)),
        ],
        hbm_out=2,
        micros=6.0,
    )
    gd, ge = call(
        outer_kernel,
        [density.shape, density.shape],
        [odd],
        [pa, pb, qa, qb, td, te, row_taps, row_shift, taps, shift, scale],
        [
            pltpu.VMEM(outer, F32),
            pltpu.VMEM(outer, F32),
            pltpu.VMEM((2, 2, rows, HALO, planes), F32),
            pltpu.VMEM((2,) + side, F32),
            pltpu.VMEM((2,) + side, F32),
            pltpu.SemaphoreType.DMA((4,)),
        ],
        hbm_in=[gd, ge],
        hbm_out=2,
        aliases={12: 0, 13: 1},
    )
    return gd, ge


def solution(mesh):
    in_specs = (
        P("groups", "screen", "depth"),
        P("groups", "screen", "depth"),
        P("groups", "depth"),
        P(("groups", "depth")),
        P("groups", "depth"),
        P(("groups", "depth")),
        P(("groups", "depth")),
        P("groups", "screen"),
    )
    out_specs = (P("groups", "screen", "depth"), P("groups", "screen", "depth"))
    return jax.shard_map(
        on_device, mesh=mesh, in_specs=in_specs, out_specs=out_specs, check_vma=False
    )
```

```python
import functools

import jax
import jax.numpy as jnp
from jax import lax
from jax.experimental import pallas as pl
from jax.experimental.pallas import tpu as pltpu
from jax.sharding import PartitionSpec as P

HALO = 8
REACH = 6
SUB = 8
F32 = jnp.float32
BF16 = jnp.bfloat16
VMEM_LIMIT = 24 * 1024 * 1024
EDGE_LIMIT = int(24 * 1024 * 1024)
UNROLL = 4
LARGEST = 64.0


def pitch_of(columns):
    return columns + 1


def loop(count, body):
    def step(i, carry):
        body(i)
        return carry

    lax.fori_loop(0, count, step, 0, unroll=min(count, UNROLL))


def bits_of(shift):
    moved = jnp.broadcast_to(shift, (SUB, shift.shape[-1])) + REACH
    return {b: (moved & b) != 0 for b in (8, 4, 2, 1)}


def rows_of(taps):
    return [jnp.broadcast_to(taps[k : k + 1, :], (SUB, taps.shape[-1])) for k in range(4)]


def choose(mask, yes, no):
    if yes is None and no is None:
        return None
    if yes is None:
        return jnp.where(mask, 0.0, no)
    if no is None:
        return jnp.where(mask, yes, 0.0)
    return jnp.where(mask, yes, no)


def resample(get, bits, taps, indices, flipped):
    way = -1 if flipped else 1
    memo = {}

    def stage(b, i):
        if b == 16:
            key = (b, i)
            if key not in memo:
                memo[key] = get(i)
            return memo[key]
        key = (b, i)
        if key not in memo:
            memo[key] = choose(bits[b], stage(2 * b, i + way * b), stage(2 * b, i))
        return memo[key]

    for i in indices:
        total = None
        for k in range(4):
            v = stage(1, i + 7 - k if flipped else i - 7 + k)
            if v is not None:
                total = taps[k] * v if total is None else total + taps[k] * v
        yield i, total


def halves(x):
    hi = x.astype(BF16)
    lo = (x - hi.astype(F32)).astype(BF16)
    return jnp.concatenate([hi, lo], axis=1)


def scan_matrix(planes, before):
    a = lax.broadcasted_iota(jnp.int32, (2 * planes, 2 * planes), 0)
    b = lax.broadcasted_iota(jnp.int32, (2 * planes, 2 * planes), 1)
    a = jnp.where(a >= planes, a - planes, a)
    ordered = (a < b) if before else (a > b)
    return jnp.where((b >= planes) | ordered, 1.0, 0.0).astype(BF16)


def edge_kernel(where_ref, field_ref, a_ref, b_ref, left_ref, right_ref, sems):
    rows, columns, _ = field_ref.shape
    copies = [
        pltpu.make_async_copy(field_ref.at[:, pl.ds(at, HALO), :], held, sems.at[n])
        for n, (at, held) in enumerate(((0, left_ref), (columns - HALO, right_ref)))
    ]
    for c in copies:
        c.start()
    odd = where_ref[0] == 1
    for c in copies:
        c.wait()

    def body(y):
        left, right = left_ref[y], right_ref[y]
        a_ref[y] = jnp.where(odd, left, right)
        b_ref[y] = jnp.where(odd, right, left)

    loop(rows, body)


def absorbed(optical, bound):
    series = 1 / 120
    for k in (-1 / 24, 1 / 6, -1 / 2, 1.0):
        series = series * optical + k
    series = series * optical
    return series if bound <= 0.125 else jnp.where(optical < 0.125, series, 1.0 - jnp.exp(-optical))


def march(optical, matrix, bound):
    planes = optical.shape[1]
    sums = jnp.dot(halves(optical), matrix, preferred_element_type=F32)
    transmit = jnp.exp(-sums[:, :planes])
    q = transmit * absorbed(optical, bound)
    return q, transmit - q, sums[:, planes:]


def inner_kernel(
    all_planes, d_ref, e_ref, row_taps_ref, row_shift_ref, taps_ref, shift_ref, scale_ref, cotangent_ref,
    rd_ref, re_ref, q_ref, p_ref, dense_ref, weight_ref,
):
    rows, columns, planes = d_ref.shape
    row_bits = bits_of(row_shift_ref[...])
    row_taps = rows_of(row_taps_ref[...])
    pitch = pitch_of(columns)
    per = 128 // columns
    cotangent = jnp.transpose(cotangent_ref[...])
    for group in range(rows // SUB):
        at = group % per * columns
        weight_ref[group // per, :, at : at + columns] = cotangent[group * SUB : (group + 1) * SUB, :]

    def row_body(t):
        at = pl.multiple_of(t * SUB, SUB)
        for ref, out in ((d_ref, rd_ref), (e_ref, re_ref)):
            get = lambda y: ref[y, pl.ds(at, SUB), :] if 0 <= y < rows else None
            for y, v in resample(get, row_bits, row_taps, range(rows), False):
                out[pl.ds(y * pitch + at, SUB), :] = v

    loop(columns // SUB, row_body)
    bits = bits_of(shift_ref[...])
    taps = rows_of(taps_ref[...])
    scale = jnp.broadcast_to(scale_ref[...] / all_planes, (SUB, planes))
    before, after = scan_matrix(planes, True), scan_matrix(planes, False)
    dense_ref[...] = jnp.zeros_like(dense_ref)
    inside = range(HALO, columns - HALO)

    def body(group):
        y0 = group * SUB
        at = pl.multiple_of(y0, SUB)
        get = column_get(rd_ref, None, y0, columns)
        optical = jnp.concatenate([scale * v for _, v in resample(get, bits, taps, inside, False)], axis=0)
        q, n, totals = march(optical, before, LARGEST / all_planes)
        pack_totals(totals, dense_ref.at[0], group, columns, inside)
        get = column_get(re_ref, None, y0, columns)
        emission = jnp.concatenate([v for _, v in resample(get, bits, taps, inside, False)], axis=0)
        sums = jnp.dot(halves(q * emission), after, preferred_element_type=F32)
        pack_totals(sums[:, planes:], dense_ref.at[1], group, columns, inside)
        p = n * emission - sums[:, :planes]
        for i in range(len(inside)):
            q_ref[i, pl.ds(at, SUB), :] = q[i * SUB : (i + 1) * SUB]
            p_ref[i, pl.ds(at, SUB), :] = scale * p[i * SUB : (i + 1) * SUB]

    loop(rows // SUB, body)


def row_halo(odd, a_ref, b_ref, halo_ref, bits, taps):
    rows = a_ref.shape[0]
    for side in range(2):
        use_a = odd == (1 - side)
        get = lambda y: jnp.where(use_a, a_ref[y], b_ref[y]) if 0 <= y < rows else None
        for y, v in resample(get, bits, taps, range(rows), False):
            halo_ref[pl.ds(y * pitch_of(2 * HALO) + side * HALO, SUB), :] = v


def column_get(r_ref, halo_ref, y0, columns):
    pitch, side_pitch = pitch_of(columns), pitch_of(2 * HALO)

    def get(x):
        reach = 0 if halo_ref is None else HALO
        if x < -reach or x >= columns + reach:
            return None
        if x < 0:
            return halo_ref[pl.ds(y0 * side_pitch + x + HALO, SUB, stride=side_pitch), :]
        if x >= columns:
            return halo_ref[pl.ds(y0 * side_pitch + HALO + x - columns, SUB, stride=side_pitch), :]
        return r_ref[pl.ds(y0 * pitch + x, SUB, stride=pitch), :]

    return get


def pack_totals(totals, dense_ref, group, columns, inside):
    lane = lax.broadcasted_iota(jnp.int32, (SUB, 128), 1)
    per = 128 // columns
    packed = jnp.zeros((SUB, 128), F32)
    base = (group % per) * columns
    for i, x in enumerate(inside):
        packed = jnp.where(lane == base + x, totals[i * SUB : (i + 1) * SUB, :], packed)
    dense_ref[group // per] += packed


def outside_of(columns):
    return [*range(HALO), *range(columns - HALO, columns)]


def density_kernel(
    all_planes, odd_ref, rd_ref, a_ref, b_ref, inner_ref, row_taps_ref, row_shift_ref, taps_ref, shift_ref, scale_ref,
    q_ref, n_ref, qa_ref, qb_ref, dense_ref, halo_ref,
):
    odd = odd_ref[0]
    rows, planes = q_ref.shape[1:]
    columns = rd_ref.shape[0] // rows - 1
    row_halo(odd, a_ref, b_ref, halo_ref, bits_of(row_shift_ref[...]), rows_of(row_taps_ref[...]))
    bits = bits_of(shift_ref[...])
    taps = rows_of(taps_ref[...])
    scale = jnp.broadcast_to(scale_ref[...] / all_planes, (SUB, planes))
    matrix = scan_matrix(planes, True)
    dense_ref[...] = inner_ref[0]
    outside = outside_of(columns)

    def body(group):
        y0 = group * SUB
        at = pl.multiple_of(y0, SUB)
        get = column_get(rd_ref, halo_ref, y0, columns)
        optical = jnp.concatenate([scale * v for _, v in resample(get, bits, taps, outside, False)], axis=0)
        q, n, totals = march(optical, matrix, LARGEST / all_planes)
        for i in range(len(outside)):
            q_ref[i, pl.ds(at, SUB), :] = q[i * SUB : (i + 1) * SUB]
            n_ref[i, pl.ds(at, SUB), :] = n[i * SUB : (i + 1) * SUB]
        pack_totals(totals, dense_ref, group, columns, outside)

    loop(rows // SUB, body)
    for ref, at in ((qa_ref, jnp.where(odd == 1, 0, HALO)), (qb_ref, jnp.where(odd == 1, HALO, 0))):
        ref[...] = q_ref[pl.ds(at, HALO)]


def emission_kernel(
    all_planes, odd_ref, re_ref, a_ref, b_ref, q_ref, n_ref, inner_ref, optical_ref, row_taps_ref, row_shift_ref, taps_ref, shift_ref, scale_ref,
    p_ref, pa_ref, pb_ref, dense_ref, halo_ref,
):
    odd = odd_ref[0]
    rows, planes = p_ref.shape[1:]
    columns = re_ref.shape[0] // rows - 1
    row_halo(odd, a_ref, b_ref, halo_ref, bits_of(row_shift_ref[...]), rows_of(row_taps_ref[...]))
    bits = bits_of(shift_ref[...])
    taps = rows_of(taps_ref[...])
    scale = jnp.broadcast_to(scale_ref[...] / all_planes, (SUB, planes))
    matrix = scan_matrix(planes, False)
    dense_ref[0] = optical_ref[...]
    dense_ref[1] = inner_ref[1]
    outside = outside_of(columns)

    def body(group):
        y0 = group * SUB
        at = pl.multiple_of(y0, SUB)
        get = column_get(re_ref, halo_ref, y0, columns)
        pieces = [v for _, v in resample(get, bits, taps, outside, False)]
        light = jnp.concatenate([q_ref[i, pl.ds(at, SUB), :] * v for i, v in enumerate(pieces)], axis=0)
        sums = jnp.dot(halves(light), matrix, preferred_element_type=F32)
        for i, v in enumerate(pieces):
            behind = sums[i * SUB : (i + 1) * SUB, :planes]
            p_ref[i, pl.ds(at, SUB), :] = scale * (n_ref[i, pl.ds(at, SUB), :] * v - behind)
        pack_totals(sums[:, planes:], dense_ref.at[1], group, columns, outside)

    loop(rows // SUB, body)
    for ref, at in ((pa_ref, jnp.where(odd == 1, 0, HALO)), (pb_ref, jnp.where(odd == 1, HALO, 0))):
        ref[...] = p_ref[pl.ds(at, HALO)]


def merge(later, mine, other, front, back):
    (depth, light), (depth_2, light_2) = mine, other
    dim = jnp.exp(-jnp.where(later, depth_2, depth))
    joined = (depth + depth_2, jnp.where(later, light_2 + dim * light, light + dim * light_2))
    return joined, jnp.where(later, front + depth_2, front), jnp.where(later, back * dim, back + dim * light_2)


def merge_kernel(step, last, where_ref, weight_ref, mine_ref, other_ref, *refs):
    later = (where_ref[1] & (1 << step)) != 0
    outs = refs if step == 0 else refs[1:]
    for c in range(weight_ref.shape[0]):
        zero = jnp.zeros_like(weight_ref[c])
        front, back = (zero, zero) if step == 0 else (refs[0][0, c], refs[0][1, c])
        joined, front, back = merge(
            later, (mine_ref[0, c], mine_ref[1, c]), (other_ref[0, c], other_ref[1, c]), front, back
        )
        if last:
            outs[0][0, c] = weight_ref[c] * jnp.exp(-front)
            outs[0][1, c] = weight_ref[c] * back
        else:
            outs[0][0, c], outs[0][1, c] = joined
            outs[1][0, c], outs[1][1, c] = front, back


def lay(split_ref, row, dense, base, first, count):
    lane = lax.broadcasted_iota(jnp.int32, (SUB, 128), 1)
    masks = [lane == base + first + x for x in range(count)]
    hi = dense.astype(BF16).astype(F32)
    stacks = [
        jnp.concatenate([jnp.where(m, part, 0.0) for m in masks], axis=0).astype(BF16) for part in (hi, dense - hi)
    ]
    split_ref[row : row + count * SUB, :] = jnp.concatenate(stacks, axis=1)


def spread(split_ref, out_ref):
    out_ref[...] = jnp.dot(split_ref[...], jnp.ones((256, 128), BF16), preferred_element_type=F32)


def finish_rows(ref, pitch, at, bits, taps, held, out, sems):
    rows = held.shape[0]
    half = rows // 2
    copies = []
    get = lambda y: ref[pl.ds(y * pitch + at, SUB), :] if 0 <= y < rows else None
    for y, v in resample(get, bits, taps, range(rows), True):
        held[y] = v
        if y % half == half - 1:
            part = pl.ds(y + 1 - half, half)
            copies.append(pltpu.make_async_copy(held.at[part], out.at[part], sems.at[y // half]))
            copies[-1].start()
    return copies


def own_kernel(
    all_planes, p_in, q_in, p_out, q_out, own_ref, row_taps_ref, row_shift_ref, taps_ref, shift_ref, scale_ref,
    gd_ref, ge_ref, td_ref, te_ref, cd_ref, ce_ref, held_ref, split_ref, weight_ref, sems,
):
    inner, rows, planes = p_in.shape
    columns = inner + 2 * HALO
    per = 128 // columns
    groups = rows // SUB
    pitch, side_pitch = pitch_of(inner), pitch_of(2 * HALO)
    bits = bits_of(shift_ref[...])
    taps = rows_of(taps_ref[...])
    scale = jnp.broadcast_to(scale_ref[...] / all_planes, (SUB, planes))

    for group in range(groups):
        lay(split_ref, group * columns * SUB, own_ref[0, group // per], group % per * columns, 0, columns)
    spread(split_ref, weight_ref)

    for group in range(groups):
        y0 = group * SUB
        back = own_ref[1, group // per]

        def front_at(x):
            row = (group * columns + x) * SUB
            return weight_ref[row : row + SUB, :]

        def back_at(x):
            lane = group % per * columns + x
            return jnp.broadcast_to(back[:, lane : lane + 1], (SUB, 128)) * scale

        def local(inside, outside, x):
            if HALO <= x < columns - HALO:
                return inside[x - HALO, y0 : y0 + SUB, :]
            return outside[x if x < HALO else x - inner, y0 : y0 + SUB, :]

        def get_d(x):
            if not 0 <= x < columns:
                return None
            return front_at(x) * local(p_in, p_out, x) - back_at(x)

        def get_e(x):
            if not 0 <= x < columns:
                return None
            return front_at(x) * local(q_in, q_out, x)

        for get, inside, outside in ((get_d, cd_ref, td_ref), (get_e, ce_ref, te_ref)):
            for x, v in resample(get, bits, taps, range(columns), True):
                if HALO <= x < columns - HALO:
                    inside[pl.ds(y0 * pitch + x - HALO, SUB, stride=pitch), :] = v
                else:
                    to = x if x < HALO else x - inner
                    outside[pl.ds(y0 * side_pitch + to, SUB, stride=side_pitch), :] = v

    row_bits = bits_of(row_shift_ref[...])
    row_taps = rows_of(row_taps_ref[...])
    copies = []
    for f, (ref, out) in enumerate(((cd_ref, gd_ref), (ce_ref, ge_ref))):
        for t in range(inner // SUB):
            copies += finish_rows(
                ref, pitch, t * SUB, row_bits, row_taps, held_ref.at[f, t],
                out.at[:, pl.ds(HALO + t * SUB, SUB), :], sems.at[f, t],
            )
    for c in copies:
        c.wait()


def outer_kernel(
    all_planes, odd_ref, pa_ref, pb_ref, qa_ref, qb_ref, wa_ref, wb_ref, td_ref, te_ref,
    row_taps_ref, row_shift_ref, taps_ref, shift_ref, scale_ref, gd_in, ge_in,
    gd_ref, ge_ref, cd_ref, ce_ref, held_ref, split_ref, weight_ref, sems,
):
    odd = odd_ref[0]
    rows, columns, planes = gd_ref.shape
    per = 128 // columns
    groups = rows // SUB
    pitch = pitch_of(2 * HALO)
    bits = bits_of(shift_ref[...])
    taps = rows_of(taps_ref[...])
    scale = jnp.broadcast_to(scale_ref[...] / all_planes, (SUB, planes))
    use_a = (odd == 1, odd != 1)

    for side in range(2):
        for group in range(groups):
            row = (side * groups + group) * HALO * SUB
            dense = jnp.where(use_a[side], wa_ref[0, group // per], wb_ref[0, group // per])
            lay(split_ref, row, dense, group % per * columns, columns - HALO if side == 0 else 0, HALO)
    spread(split_ref, weight_ref)

    for group in range(groups):
        y0 = group * SUB
        for side in range(2):
            start = -HALO if side == 0 else HALO
            back = jnp.where(use_a[side], wa_ref[1, group // per], wb_ref[1, group // per])

            def front_at(i):
                row = ((side * groups + group) * HALO + i) * SUB
                return weight_ref[row : row + SUB, :]

            def back_at(i):
                lane = group % per * columns + i + (columns - HALO if side == 0 else 0)
                return jnp.broadcast_to(back[:, lane : lane + 1], (SUB, 128)) * scale

            def get_d(x):
                i = x - start
                if not 0 <= i < HALO:
                    return None
                v = jnp.where(use_a[side], pa_ref[i, y0 : y0 + SUB, :], pb_ref[i, y0 : y0 + SUB, :])
                return front_at(i) * v - back_at(i)

            def get_e(x):
                i = x - start
                if not 0 <= i < HALO:
                    return None
                v = jnp.where(use_a[side], qa_ref[i, y0 : y0 + SUB, :], qb_ref[i, y0 : y0 + SUB, :])
                return front_at(i) * v

            for get, ref, out in ((get_d, td_ref, cd_ref), (get_e, te_ref, ce_ref)):
                for x, v in resample(get, bits, taps, range(HALO), True):
                    at = pl.ds(y0 * pitch + side * HALO + x, SUB, stride=pitch)
                    out[at, :] = ref[at, :] if v is None else ref[at, :] + v

    row_bits = bits_of(row_shift_ref[...])
    row_taps = rows_of(row_taps_ref[...])
    copies = []
    for f, (ref, out) in enumerate(((cd_ref, gd_ref), (ce_ref, ge_ref))):
        for side in range(2):
            copies += finish_rows(
                ref, pitch, side * HALO, row_bits, row_taps, held_ref.at[f, side],
                out.at[:, pl.ds(side * (columns - HALO), HALO), :], sems.at[f, side],
            )
    for c in copies:
        c.wait()


def near(value):
    big = value.size >= 1 << 16
    return pltpu.with_memory_space_constraint(value, pltpu.VMEM) if big else value


def call(kernel, outs, scalars, vmem, scratch=(), hbm_in=(), hbm_out=0, aliases=None, micros=2.0, limit=VMEM_LIMIT):
    whole, far = pl.BlockSpec(memory_space=pltpu.VMEM), pl.BlockSpec(memory_space=pl.ANY)
    return pl.pallas_call(
        kernel,
        out_shape=[jax.ShapeDtypeStruct(s, F32) if i < hbm_out else pltpu.VMEM(s, F32) for i, s in enumerate(outs)],
        in_specs=[pl.BlockSpec(memory_space=pltpu.SMEM)] * len(scalars)
        + [whole] * len(vmem)
        + [far] * len(hbm_in),
        out_specs=[far] * hbm_out + [whole] * (len(outs) - hbm_out),
        scratch_shapes=list(scratch),
        input_output_aliases=aliases or {},
        compiler_params=pltpu.CompilerParams(vmem_limit_bytes=limit),
        cost_estimate=pl.CostEstimate(
            flops=int(micros * 1e6), bytes_accessed=int(micros * 3.0e6), transcendentals=0
        ),
    )(*scalars, *[near(v) for v in vmem], *[pltpu.with_memory_space_constraint(v, pltpu.HBM) for v in hbm_in])


def swap(value, axis, parity):
    count = lax.axis_size(axis)
    pairs = []
    for i in range(parity, count - 1, 2):
        pairs += [(i, i + 1), (i + 1, i)]
    return lax.ppermute(value, axis, pairs)


def on_device(density, emission, taps, shift, row_taps, row_shift, step_length, cotangent):
    rows, columns, planes = density.shape
    slabs = lax.axis_size("depth")
    all_planes = planes * slabs
    per = 128 // columns
    chunks = rows // SUB // per
    shift, row_shift = shift[None, :], row_shift[None, :]
    scale = step_length[None, :]
    place = jnp.stack([lax.axis_index("screen") % 2, lax.axis_index("depth")]).astype(jnp.int32)
    where = jnp.broadcast_to(place[:, None, None], (2, SUB, 128))
    edge = (rows, HALO, planes)
    sides = []
    for field in (density, emission):
        a, b = call(
            edge_kernel,
            [edge] * 2,
            [],
            [where],
            [pltpu.VMEM(edge, F32), pltpu.VMEM(edge, F32), pltpu.SemaphoreType.DMA((2,))],
            hbm_in=[field],
            micros=0.2,
        )
        sides.append((swap(a, "screen", 0), swap(b, "screen", 1)))
    (da, db), (ea, eb) = sides
    flat = (rows * pitch_of(columns), planes)
    inside = (columns - 2 * HALO, rows, planes)
    outside = (2 * HALO, rows, planes)
    side = (HALO, rows, planes)
    dense = (chunks, SUB, 128)
    rd, re, q_in, p_in, inner_sums, weight = call(
        functools.partial(inner_kernel, all_planes),
        [flat, flat, inside, inside, (2,) + dense, dense],
        [],
        [density, emission, row_taps, row_shift, taps, shift, scale, cotangent.T],
        micros=3.0,
    )
    outer = (rows * pitch_of(2 * HALO), planes)
    q_out, n_out, qa, qb, slab_optical = call(
        functools.partial(density_kernel, all_planes),
        [outside, outside, side, side, dense],
        [place],
        [rd, da, db, inner_sums, row_taps, row_shift, taps, shift, scale],
        [pltpu.VMEM(outer, F32)],
    )
    qa, qb = swap(qa, "screen", 0), swap(qb, "screen", 1)
    p_out, pa, pb, state = call(
        functools.partial(emission_kernel, all_planes),
        [outside, side, side, (2,) + dense],
        [place],
        [re, ea, eb, q_out, n_out, inner_sums, slab_optical, row_taps, row_shift, taps, shift, scale],
        [pltpu.VMEM(outer, F32)],
        micros=6.0,
    )
    rounds = slabs.bit_length() - 1
    assert slabs == 1 << rounds and rounds
    sums = (2,) + dense
    around = []
    for step in range(rounds):
        last = step == rounds - 1
        if last:
            pa, pb = swap(pa, "screen", 0), swap(pb, "screen", 1)
        other = lax.ppermute(state, "depth", [(i, i ^ (1 << step)) for i in range(slabs)])
        state, *around = call(
            functools.partial(merge_kernel, step, last),
            [sums] * (1 if last else 2),
            [],
            [where, weight, state, other] + around,
            micros=0.1,
        )
    own, qa, qb = lax.optimization_barrier((state, qa, qb))
    wa, wb = swap(own, "screen", 0), swap(own, "screen", 1)
    inner = (rows * pitch_of(columns - 2 * HALO), planes)
    halves_of = rows * columns
    gd, ge, td, te = call(
        functools.partial(own_kernel, all_planes),
        [density.shape, density.shape, outer, outer],
        [],
        [p_in, q_in, p_out, q_out, own, row_taps, row_shift, taps, shift, scale],
        [
            pltpu.VMEM(inner, F32),
            pltpu.VMEM(inner, F32),
            pltpu.VMEM((2, (columns - 2 * HALO) // SUB, rows, SUB, planes), F32),
            pltpu.VMEM((halves_of, 256), BF16),
            pltpu.VMEM((halves_of, planes), F32),
            pltpu.SemaphoreType.DMA((2, (columns - 2 * HALO) // SUB, 2)),
        ],
        hbm_out=2,
        micros=6.0,
    )
    halves_of = rows * HALO * 2
    gd, ge = call(
        functools.partial(outer_kernel, all_planes),
        [density.shape, density.shape],
        [place],
        [pa, pb, qa, qb, wa, wb, td, te, row_taps, row_shift, taps, shift, scale],
        [
            pltpu.VMEM(outer, F32),
            pltpu.VMEM(outer, F32),
            pltpu.VMEM((2, 2, rows, HALO, planes), F32),
            pltpu.VMEM((halves_of, 256), BF16),
            pltpu.VMEM((halves_of, planes), F32),
            pltpu.SemaphoreType.DMA((2, 2, 2)),
        ],
        hbm_in=[gd, ge],
        hbm_out=2,
        aliases={14: 0, 15: 1},
    )
    return gd, ge


def solution(mesh):
    in_specs = (
        P("groups", "screen", "depth"),
        P("groups", "screen", "depth"),
        P("groups", "depth"),
        P(("groups", "depth")),
        P("groups", "depth"),
        P(("groups", "depth")),
        P(("groups", "depth")),
        P("groups", "screen"),
    )
    out_specs = (P("groups", "screen", "depth"), P("groups", "screen", "depth"))
    return jax.shard_map(
        on_device, mesh=mesh, in_specs=in_specs, out_specs=out_specs, check_vma=False
    )
```

```python
import functools

import jax
import jax.numpy as jnp
from jax import lax
from jax.experimental import pallas as pl
from jax.experimental.pallas import tpu as pltpu
from jax.sharding import PartitionSpec as P

HALO = 8
REACH = 6
SUB = 8
F32 = jnp.float32
BF16 = jnp.bfloat16
VMEM_LIMIT = 24 * 1024 * 1024
EDGE_LIMIT = int(24 * 1024 * 1024)
UNROLL = 4
LARGEST = 64.0


def pitch_of(columns):
    return columns + 1


def loop(count, body):
    def step(i, carry):
        body(i)
        return carry

    lax.fori_loop(0, count, step, 0, unroll=min(count, UNROLL))


def bits_of(shift):
    moved = jnp.broadcast_to(shift, (SUB, shift.shape[-1])) + REACH
    return {b: (moved & b) != 0 for b in (8, 4, 2, 1)}


def rows_of(taps):
    return [jnp.broadcast_to(taps[k : k + 1, :], (SUB, taps.shape[-1])) for k in range(4)]


def choose(mask, yes, no):
    if yes is None and no is None:
        return None
    if yes is None:
        return jnp.where(mask, 0.0, no)
    if no is None:
        return jnp.where(mask, yes, 0.0)
    return jnp.where(mask, yes, no)


def resample(get, bits, taps, indices, flipped):
    way = -1 if flipped else 1
    memo = {}

    def stage(b, i):
        if b == 16:
            key = (b, i)
            if key not in memo:
                memo[key] = get(i)
            return memo[key]
        key = (b, i)
        if key not in memo:
            memo[key] = choose(bits[b], stage(2 * b, i + way * b), stage(2 * b, i))
        return memo[key]

    for i in indices:
        total = None
        for k in range(4):
            v = stage(1, i + 7 - k if flipped else i - 7 + k)
            if v is not None:
                total = taps[k] * v if total is None else total + taps[k] * v
        yield i, total


def halves(x):
    hi = x.astype(BF16)
    lo = (x - hi.astype(F32)).astype(BF16)
    return jnp.concatenate([hi, lo], axis=1)


def scan_matrix(planes, before):
    a = lax.broadcasted_iota(jnp.int32, (2 * planes, 2 * planes), 0)
    b = lax.broadcasted_iota(jnp.int32, (2 * planes, 2 * planes), 1)
    a = jnp.where(a >= planes, a - planes, a)
    ordered = (a < b) if before else (a > b)
    return jnp.where((b >= planes) | ordered, 1.0, 0.0).astype(BF16)


def edge_kernel(where_ref, field_ref, a_ref, b_ref, left_ref, right_ref, sems):
    rows, columns, _ = field_ref.shape
    copies = [
        pltpu.make_async_copy(field_ref.at[:, pl.ds(at, HALO), :], held, sems.at[n])
        for n, (at, held) in enumerate(((0, left_ref), (columns - HALO, right_ref)))
    ]
    for c in copies:
        c.start()
    odd = where_ref[0] == 1
    for c in copies:
        c.wait()

    def body(y):
        left, right = left_ref[y], right_ref[y]
        a_ref[y] = jnp.where(odd, left, right)
        b_ref[y] = jnp.where(odd, right, left)

    loop(rows, body)


def absorbed(optical, bound):
    series = 1 / 120
    for k in (-1 / 24, 1 / 6, -1 / 2, 1.0):
        series = series * optical + k
    series = series * optical
    return series if bound <= 0.125 else jnp.where(optical < 0.125, series, 1.0 - jnp.exp(-optical))


def march(optical, matrix, bound):
    planes = optical.shape[1]
    sums = jnp.dot(halves(optical), matrix, preferred_element_type=F32)
    transmit = jnp.exp(-sums[:, :planes])
    q = transmit * absorbed(optical, bound)
    return q, transmit - q, sums[:, planes:]


def inner_kernel(
    all_planes, d_ref, e_ref, row_taps_ref, row_shift_ref, taps_ref, shift_ref, scale_ref, cotangent_ref,
    rd_ref, re_ref, q_ref, p_ref, dense_ref, weight_ref,
):
    rows, columns, planes = d_ref.shape
    row_bits = bits_of(row_shift_ref[...])
    row_taps = rows_of(row_taps_ref[...])
    pitch = pitch_of(columns)
    per = 128 // columns
    cotangent = jnp.transpose(cotangent_ref[...])
    for group in range(rows // SUB):
        at = group % per * columns
        weight_ref[group // per, :, at : at + columns] = cotangent[group * SUB : (group + 1) * SUB, :]

    def row_body(t):
        at = pl.multiple_of(t * SUB, SUB)
        for ref, out in ((d_ref, rd_ref), (e_ref, re_ref)):
            get = lambda y: ref[y, pl.ds(at, SUB), :] if 0 <= y < rows else None
            for y, v in resample(get, row_bits, row_taps, range(rows), False):
                out[pl.ds(y * pitch + at, SUB), :] = v

    loop(columns // SUB, row_body)
    bits = bits_of(shift_ref[...])
    taps = rows_of(taps_ref[...])
    scale = jnp.broadcast_to(scale_ref[...] / all_planes, (SUB, planes))
    before, after = scan_matrix(planes, True), scan_matrix(planes, False)
    dense_ref[...] = jnp.zeros_like(dense_ref)
    inside = range(HALO, columns - HALO)

    def body(group):
        y0 = group * SUB
        at = pl.multiple_of(y0, SUB)
        get = column_get(rd_ref, None, y0, columns)
        optical = jnp.concatenate([scale * v for _, v in resample(get, bits, taps, inside, False)], axis=0)
        q, n, totals = march(optical, before, LARGEST / all_planes)
        pack_totals(totals, dense_ref.at[0], group, columns, inside)
        get = column_get(re_ref, None, y0, columns)
        emission = jnp.concatenate([v for _, v in resample(get, bits, taps, inside, False)], axis=0)
        sums = jnp.dot(halves(q * emission), after, preferred_element_type=F32)
        pack_totals(sums[:, planes:], dense_ref.at[1], group, columns, inside)
        p = n * emission - sums[:, :planes]
        for i in range(len(inside)):
            q_ref[i, pl.ds(at, SUB), :] = q[i * SUB : (i + 1) * SUB]
            p_ref[i, pl.ds(at, SUB), :] = scale * p[i * SUB : (i + 1) * SUB]

    loop(rows // SUB, body)


def row_halo(odd, a_ref, b_ref, halo_ref, bits, taps):
    rows = a_ref.shape[0]
    for side in range(2):
        use_a = odd if side == 0 else ~odd
        get = lambda y: jnp.where(use_a, a_ref[y], b_ref[y]) if 0 <= y < rows else None
        for y, v in resample(get, bits, taps, range(rows), False):
            halo_ref[pl.ds(y * pitch_of(2 * HALO) + side * HALO, SUB), :] = v


def column_get(r_ref, halo_ref, y0, columns):
    pitch, side_pitch = pitch_of(columns), pitch_of(2 * HALO)

    def get(x):
        reach = 0 if halo_ref is None else HALO
        if x < -reach or x >= columns + reach:
            return None
        if x < 0:
            return halo_ref[pl.ds(y0 * side_pitch + x + HALO, SUB, stride=side_pitch), :]
        if x >= columns:
            return halo_ref[pl.ds(y0 * side_pitch + HALO + x - columns, SUB, stride=side_pitch), :]
        return r_ref[pl.ds(y0 * pitch + x, SUB, stride=pitch), :]

    return get


def pack_totals(totals, dense_ref, group, columns, inside):
    lane = lax.broadcasted_iota(jnp.int32, (SUB, 128), 1)
    per = 128 // columns
    packed = jnp.zeros((SUB, 128), F32)
    base = (group % per) * columns
    for i, x in enumerate(inside):
        packed = jnp.where(lane == base + x, totals[i * SUB : (i + 1) * SUB, :], packed)
    dense_ref[group // per] += packed


def outside_of(columns):
    return [*range(HALO), *range(columns - HALO, columns)]


def split_edges(odd, refs, a_ref, b_ref):
    rows = refs[0].shape[1]

    def body(group):
        at = pl.ds(pl.multiple_of(group * SUB, SUB), SUB)
        for n, ref in enumerate(refs):
            for i in range(HALO):
                left, right = ref[i, at, :], ref[HALO + i, at, :]
                a_ref[n * HALO + i, at, :] = jnp.where(odd, left, right)
                b_ref[n * HALO + i, at, :] = jnp.where(odd, right, left)

    loop(rows // SUB, body)


def density_kernel(
    all_planes, odd_ref, rd_ref, a_ref, b_ref, inner_ref, row_taps_ref, row_shift_ref, taps_ref, shift_ref, scale_ref,
    q_ref, n_ref, dense_ref, halo_ref,
):
    odd = odd_ref[0] == 1
    rows, planes = q_ref.shape[1:]
    columns = rd_ref.shape[0] // rows - 1
    row_halo(odd, a_ref, b_ref, halo_ref, bits_of(row_shift_ref[...]), rows_of(row_taps_ref[...]))
    bits = bits_of(shift_ref[...])
    taps = rows_of(taps_ref[...])
    scale = jnp.broadcast_to(scale_ref[...] / all_planes, (SUB, planes))
    matrix = scan_matrix(planes, True)
    dense_ref[...] = inner_ref[0]
    outside = outside_of(columns)

    def body(group):
        y0 = group * SUB
        at = pl.multiple_of(y0, SUB)
        get = column_get(rd_ref, halo_ref, y0, columns)
        optical = jnp.concatenate([scale * v for _, v in resample(get, bits, taps, outside, False)], axis=0)
        q, n, totals = march(optical, matrix, LARGEST / all_planes)
        for i in range(len(outside)):
            q_ref[i, pl.ds(at, SUB), :] = q[i * SUB : (i + 1) * SUB]
            n_ref[i, pl.ds(at, SUB), :] = n[i * SUB : (i + 1) * SUB]
        pack_totals(totals, dense_ref, group, columns, outside)

    loop(rows // SUB, body)


def emission_kernel(
    all_planes, odd_ref, re_ref, a_ref, b_ref, q_ref, n_ref, inner_ref, optical_ref, row_taps_ref, row_shift_ref, taps_ref, shift_ref, scale_ref,
    p_ref, pa_ref, pb_ref, dense_ref, halo_ref,
):
    odd = odd_ref[0] == 1
    rows, planes = p_ref.shape[1:]
    columns = re_ref.shape[0] // rows - 1
    row_halo(odd, a_ref, b_ref, halo_ref, bits_of(row_shift_ref[...]), rows_of(row_taps_ref[...]))
    bits = bits_of(shift_ref[...])
    taps = rows_of(taps_ref[...])
    scale = jnp.broadcast_to(scale_ref[...] / all_planes, (SUB, planes))
    matrix = scan_matrix(planes, False)
    dense_ref[0] = optical_ref[...]
    dense_ref[1] = inner_ref[1]
    outside = outside_of(columns)

    def body(group):
        y0 = group * SUB
        at = pl.multiple_of(y0, SUB)
        get = column_get(re_ref, halo_ref, y0, columns)
        pieces = [v for _, v in resample(get, bits, taps, outside, False)]
        light = jnp.concatenate([q_ref[i, pl.ds(at, SUB), :] * v for i, v in enumerate(pieces)], axis=0)
        sums = jnp.dot(halves(light), matrix, preferred_element_type=F32)
        for i, v in enumerate(pieces):
            behind = sums[i * SUB : (i + 1) * SUB, :planes]
            p_ref[i, pl.ds(at, SUB), :] = scale * (n_ref[i, pl.ds(at, SUB), :] * v - behind)
        pack_totals(sums[:, planes:], dense_ref.at[1], group, columns, outside)

    loop(rows // SUB, body)
    split_edges(odd, (p_ref, q_ref), pa_ref, pb_ref)


def join_kernel(count, where_ref, weight_ref, *refs):
    sums, out_ref = refs[:count], refs[count]
    mine = where_ref[1]
    for c in range(weight_ref.shape[0]):
        front = jnp.zeros_like(weight_ref[c])
        for ahead in range(1, count):
            front += jnp.where(mine + ahead >= count, sums[ahead][0, c], 0.0)
        running = front + sums[0][0, c]
        back = jnp.zeros_like(front)
        for ahead in range(1, count):
            there = mine + ahead < count
            back += jnp.where(there, jnp.exp(-running) * sums[ahead][1, c], 0.0)
            running += jnp.where(there, sums[ahead][0, c], 0.0)
        out_ref[0, c] = weight_ref[c] * jnp.exp(-front)
        out_ref[1, c] = weight_ref[c] * back


def lay(split_ref, row, dense, base, first, count):
    lane = lax.broadcasted_iota(jnp.int32, (SUB, 128), 1)
    masks = [lane == base + first + x for x in range(count)]
    hi = dense.astype(BF16).astype(F32)
    stacks = [
        jnp.concatenate([jnp.where(m, part, 0.0) for m in masks], axis=0).astype(BF16) for part in (hi, dense - hi)
    ]
    split_ref[row : row + count * SUB, :] = jnp.concatenate(stacks, axis=1)


def spread(split_ref, out_ref):
    out_ref[...] = jnp.dot(split_ref[...], jnp.ones((256, 128), BF16), preferred_element_type=F32)


def finish_rows(ref, pitch, at, bits, taps, held, out, sems):
    rows = held.shape[0]
    half = rows // 2
    copies = []
    get = lambda y: ref[pl.ds(y * pitch + at, SUB), :] if 0 <= y < rows else None
    for y, v in resample(get, bits, taps, range(rows), True):
        held[y] = v
        if y % half == half - 1:
            part = pl.ds(y + 1 - half, half)
            copies.append(pltpu.make_async_copy(held.at[part], out.at[part], sems.at[y // half]))
            copies[-1].start()
    return copies


def own_kernel(
    all_planes, p_in, q_in, p_out, q_out, own_ref, row_taps_ref, row_shift_ref, taps_ref, shift_ref, scale_ref,
    gd_ref, ge_ref, td_ref, te_ref, cd_ref, ce_ref, held_ref, split_ref, weight_ref, sems,
):
    inner, rows, planes = p_in.shape
    columns = inner + 2 * HALO
    per = 128 // columns
    groups = rows // SUB
    pitch, side_pitch = pitch_of(inner), pitch_of(2 * HALO)
    bits = bits_of(shift_ref[...])
    taps = rows_of(taps_ref[...])
    scale = jnp.broadcast_to(scale_ref[...] / all_planes, (SUB, planes))

    for group in range(groups):
        lay(split_ref, group * columns * SUB, own_ref[0, group // per], group % per * columns, 0, columns)
    spread(split_ref, weight_ref)

    for group in range(groups):
        y0 = group * SUB
        back = own_ref[1, group // per]

        def front_at(x):
            row = (group * columns + x) * SUB
            return weight_ref[row : row + SUB, :]

        def back_at(x):
            lane = group % per * columns + x
            return jnp.broadcast_to(back[:, lane : lane + 1], (SUB, 128)) * scale

        def local(inside, outside, x):
            if HALO <= x < columns - HALO:
                return inside[x - HALO, y0 : y0 + SUB, :]
            return outside[x if x < HALO else x - inner, y0 : y0 + SUB, :]

        def get_d(x):
            if not 0 <= x < columns:
                return None
            return front_at(x) * local(p_in, p_out, x) - back_at(x)

        def get_e(x):
            if not 0 <= x < columns:
                return None
            return front_at(x) * local(q_in, q_out, x)

        for get, inside, outside in ((get_d, cd_ref, td_ref), (get_e, ce_ref, te_ref)):
            for x, v in resample(get, bits, taps, range(columns), True):
                if HALO <= x < columns - HALO:
                    inside[pl.ds(y0 * pitch + x - HALO, SUB, stride=pitch), :] = v
                else:
                    to = x if x < HALO else x - inner
                    outside[pl.ds(y0 * side_pitch + to, SUB, stride=side_pitch), :] = v

    row_bits = bits_of(row_shift_ref[...])
    row_taps = rows_of(row_taps_ref[...])
    copies = []
    for f, (ref, out) in enumerate(((cd_ref, gd_ref), (ce_ref, ge_ref))):
        for t in range(inner // SUB):
            copies += finish_rows(
                ref, pitch, t * SUB, row_bits, row_taps, held_ref.at[f, t],
                out.at[:, pl.ds(HALO + t * SUB, SUB), :], sems.at[f, t],
            )
    for c in copies:
        c.wait()


def outer_kernel(
    all_planes, odd_ref, pa_ref, pb_ref, wb_ref, wa_ref, td_ref, te_ref,
    row_taps_ref, row_shift_ref, taps_ref, shift_ref, scale_ref, gd_in, ge_in,
    gd_ref, ge_ref, cd_ref, ce_ref, held_ref, split_ref, weight_ref, sems,
):
    odd = odd_ref[0] == 1
    rows, columns, planes = gd_ref.shape
    per = 128 // columns
    groups = rows // SUB
    pitch = pitch_of(2 * HALO)
    bits = bits_of(shift_ref[...])
    taps = rows_of(taps_ref[...])
    scale = jnp.broadcast_to(scale_ref[...] / all_planes, (SUB, planes))
    use_a = (odd, ~odd)

    for side in range(2):
        for group in range(groups):
            row = (side * groups + group) * HALO * SUB
            dense = jnp.where(use_a[side], wa_ref[0, group // per], wb_ref[0, group // per])
            lay(split_ref, row, dense, group % per * columns, columns - HALO if side == 0 else 0, HALO)
    spread(split_ref, weight_ref)

    for group in range(groups):
        y0 = group * SUB
        for side in range(2):
            start = -HALO if side == 0 else HALO
            back = jnp.where(use_a[side], wa_ref[1, group // per], wb_ref[1, group // per])

            def front_at(i):
                row = ((side * groups + group) * HALO + i) * SUB
                return weight_ref[row : row + SUB, :]

            def back_at(i):
                lane = group % per * columns + i + (columns - HALO if side == 0 else 0)
                return jnp.broadcast_to(back[:, lane : lane + 1], (SUB, 128)) * scale

            def get_d(x):
                i = x - start
                if not 0 <= i < HALO:
                    return None
                v = jnp.where(use_a[side], pa_ref[i, y0 : y0 + SUB, :], pb_ref[i, y0 : y0 + SUB, :])
                return front_at(i) * v - back_at(i)

            def get_e(x):
                i = x - start
                if not 0 <= i < HALO:
                    return None
                v = jnp.where(use_a[side], pa_ref[HALO + i, y0 : y0 + SUB, :], pb_ref[HALO + i, y0 : y0 + SUB, :])
                return front_at(i) * v

            for get, ref, out in ((get_d, td_ref, cd_ref), (get_e, te_ref, ce_ref)):
                for x, v in resample(get, bits, taps, range(HALO), True):
                    at = pl.ds(y0 * pitch + side * HALO + x, SUB, stride=pitch)
                    out[at, :] = ref[at, :] if v is None else ref[at, :] + v

    row_bits = bits_of(row_shift_ref[...])
    row_taps = rows_of(row_taps_ref[...])
    copies = []
    for f, (ref, out) in enumerate(((cd_ref, gd_ref), (ce_ref, ge_ref))):
        for side in range(2):
            copies += finish_rows(
                ref, pitch, side * HALO, row_bits, row_taps, held_ref.at[f, side],
                out.at[:, pl.ds(side * (columns - HALO), HALO), :], sems.at[f, side],
            )
    for c in copies:
        c.wait()


def near(value):
    big = value.size >= 1 << 16
    return pltpu.with_memory_space_constraint(value, pltpu.VMEM) if big else value


def call(kernel, outs, scalars, vmem, scratch=(), hbm_in=(), hbm_out=0, aliases=None, micros=2.0, limit=VMEM_LIMIT):
    whole, far = pl.BlockSpec(memory_space=pltpu.VMEM), pl.BlockSpec(memory_space=pl.ANY)
    return pl.pallas_call(
        kernel,
        out_shape=[jax.ShapeDtypeStruct(s, F32) if i < hbm_out else pltpu.VMEM(s, F32) for i, s in enumerate(outs)],
        in_specs=[pl.BlockSpec(memory_space=pltpu.SMEM)] * len(scalars)
        + [whole] * len(vmem)
        + [far] * len(hbm_in),
        out_specs=[far] * hbm_out + [whole] * (len(outs) - hbm_out),
        scratch_shapes=list(scratch),
        input_output_aliases=aliases or {},
        compiler_params=pltpu.CompilerParams(vmem_limit_bytes=limit),
        cost_estimate=pl.CostEstimate(
            flops=int(micros * 1e6), bytes_accessed=int(micros * 3.0e6), transcendentals=0
        ),
    )(*scalars, *[near(v) for v in vmem], *[pltpu.with_memory_space_constraint(v, pltpu.HBM) for v in hbm_in])


def swap(value, axis, parity):
    count = lax.axis_size(axis)
    pairs = []
    for i in range(parity, count - 1, 2):
        pairs += [(i, i + 1), (i + 1, i)]
    return lax.ppermute(value, axis, pairs)


def on_device(density, emission, taps, shift, row_taps, row_shift, step_length, cotangent):
    rows, columns, planes = density.shape
    slabs = lax.axis_size("depth")
    all_planes = planes * slabs
    per = 128 // columns
    chunks = rows // SUB // per
    shift, row_shift = shift[None, :], row_shift[None, :]
    scale = step_length[None, :]
    place = jnp.stack([lax.axis_index("screen") % 2, lax.axis_index("depth")]).astype(jnp.int32)
    where = jnp.broadcast_to(place[:, None, None], (2, SUB, 128))
    edge = (rows, HALO, planes)
    sides = []
    for field in (density, emission):
        a, b = call(
            edge_kernel,
            [edge] * 2,
            [],
            [where],
            [pltpu.VMEM(edge, F32), pltpu.VMEM(edge, F32), pltpu.SemaphoreType.DMA((2,))],
            hbm_in=[field],
            micros=0.2,
        )
        sides.append((swap(a, "screen", 0), swap(b, "screen", 1)))
    (da, db), (ea, eb) = sides
    flat = (rows * pitch_of(columns), planes)
    inside = (columns - 2 * HALO, rows, planes)
    outside = (2 * HALO, rows, planes)
    side = (HALO, rows, planes)
    dense = (chunks, SUB, 128)
    rd, re, q_in, p_in, inner_sums, weight = call(
        functools.partial(inner_kernel, all_planes),
        [flat, flat, inside, inside, (2,) + dense, dense],
        [],
        [density, emission, row_taps, row_shift, taps, shift, scale, cotangent.T],
        micros=3.0,
    )
    outer = (rows * pitch_of(2 * HALO), planes)
    q_out, n_out, slab_optical = call(
        functools.partial(density_kernel, all_planes),
        [outside, outside, dense],
        [],
        [where, rd, da, db, inner_sums, row_taps, row_shift, taps, shift, scale],
        [pltpu.VMEM(outer, F32)],
    )
    p_out, pa, pb, state = call(
        functools.partial(emission_kernel, all_planes),
        [outside, outside, outside, (2,) + dense],
        [],
        [where, re, ea, eb, q_out, n_out, inner_sums, slab_optical, row_taps, row_shift, taps, shift, scale],
        [pltpu.VMEM(outer, F32)],
        micros=6.0,
    )
    pa, pb = swap(pa, "screen", 0), swap(pb, "screen", 1)
    ahead = [state] + [
        lax.ppermute(state, "depth", [((i + e) % slabs, i) for i in range(slabs)]) for e in range(1, slabs)
    ]
    (own,) = call(
        functools.partial(join_kernel, slabs), [(2,) + dense], [], [where, weight] + ahead, micros=0.1
    )
    wa, wb = swap(own, "screen", 0), swap(own, "screen", 1)
    inner = (rows * pitch_of(columns - 2 * HALO), planes)
    halves_of = rows * columns
    gd, ge, td, te = call(
        functools.partial(own_kernel, all_planes),
        [density.shape, density.shape, outer, outer],
        [],
        [p_in, q_in, p_out, q_out, own, row_taps, row_shift, taps, shift, scale],
        [
            pltpu.VMEM(inner, F32),
            pltpu.VMEM(inner, F32),
            pltpu.VMEM((2, (columns - 2 * HALO) // SUB, rows, SUB, planes), F32),
            pltpu.VMEM((halves_of, 256), BF16),
            pltpu.VMEM((halves_of, planes), F32),
            pltpu.SemaphoreType.DMA((2, (columns - 2 * HALO) // SUB, 2)),
        ],
        hbm_out=2,
        micros=6.0,
    )
    halves_of = rows * HALO * 2
    gd, ge = call(
        functools.partial(outer_kernel, all_planes),
        [density.shape, density.shape],
        [],
        [where, pa, pb, wb, wa, td, te, row_taps, row_shift, taps, shift, scale],
        [
            pltpu.VMEM(outer, F32),
            pltpu.VMEM(outer, F32),
            pltpu.VMEM((2, 2, rows, HALO, planes), F32),
            pltpu.VMEM((halves_of, 256), BF16),
            pltpu.VMEM((halves_of, planes), F32),
            pltpu.SemaphoreType.DMA((2, 2, 2)),
        ],
        hbm_in=[gd, ge],
        hbm_out=2,
        aliases={12: 0, 13: 1},
    )
    return gd, ge


def solution(mesh):
    in_specs = (
        P("groups", "screen", "depth"),
        P("groups", "screen", "depth"),
        P("groups", "depth"),
        P(("groups", "depth")),
        P("groups", "depth"),
        P(("groups", "depth")),
        P(("groups", "depth")),
        P("groups", "screen"),
    )
    out_specs = (P("groups", "screen", "depth"), P("groups", "screen", "depth"))
    return jax.shard_map(
        on_device, mesh=mesh, in_specs=in_specs, out_specs=out_specs, check_vma=False
    )
```

```python
import functools

import jax
import jax.numpy as jnp
from jax import lax
from jax.experimental import pallas as pl
from jax.experimental.pallas import tpu as pltpu
from jax.sharding import PartitionSpec as P

HALO = 8
REACH = 6
SUB = 8
F32 = jnp.float32
BF16 = jnp.bfloat16
VMEM_LIMIT = 24 * 1024 * 1024
EDGE_LIMIT = int(24 * 1024 * 1024)
UNROLL = 8
LARGEST = 64.0


def pitch_of(columns):
    return columns + 1


def loop(count, body):
    def step(i, carry):
        body(i)
        return carry

    lax.fori_loop(0, count, step, 0, unroll=min(count, UNROLL))


def bits_of(shift):
    moved = jnp.broadcast_to(shift, (SUB, shift.shape[-1])) + REACH
    return {b: (moved & b) != 0 for b in (8, 4, 2, 1)}


def rows_of(taps):
    return [jnp.broadcast_to(taps[k : k + 1, :], (SUB, taps.shape[-1])) for k in range(4)]


def choose(mask, yes, no):
    if yes is None and no is None:
        return None
    if yes is None:
        return jnp.where(mask, 0.0, no)
    if no is None:
        return jnp.where(mask, yes, 0.0)
    return jnp.where(mask, yes, no)


def resample(get, bits, taps, indices, flipped):
    way = -1 if flipped else 1
    memo = {}

    def stage(b, i):
        if b == 16:
            key = (b, i)
            if key not in memo:
                memo[key] = get(i)
            return memo[key]
        key = (b, i)
        if key not in memo:
            memo[key] = choose(bits[b], stage(2 * b, i + way * b), stage(2 * b, i))
        return memo[key]

    for i in indices:
        total = None
        for k in range(4):
            v = stage(1, i + 7 - k if flipped else i - 7 + k)
            if v is not None:
                total = taps[k] * v if total is None else total + taps[k] * v
        yield i, total


def halves(x):
    hi = x.astype(BF16)
    lo = (x - hi.astype(F32)).astype(BF16)
    return jnp.concatenate([hi, lo], axis=1)


def scan_matrix(planes, before):
    a = lax.broadcasted_iota(jnp.int32, (2 * planes, 2 * planes), 0)
    b = lax.broadcasted_iota(jnp.int32, (2 * planes, 2 * planes), 1)
    a = jnp.where(a >= planes, a - planes, a)
    ordered = (a < b) if before else (a > b)
    return jnp.where((b >= planes) | ordered, 1.0, 0.0).astype(BF16)


def edge_kernel(where_ref, field_ref, a_ref, b_ref, left_ref, right_ref, sems):
    rows, columns, _ = field_ref.shape
    copies = [
        pltpu.make_async_copy(field_ref.at[:, pl.ds(at, HALO), :], held, sems.at[n])
        for n, (at, held) in enumerate(((0, left_ref), (columns - HALO, right_ref)))
    ]
    for c in copies:
        c.start()
    odd = where_ref[0] == 1
    for c in copies:
        c.wait()

    def body(y):
        left, right = left_ref[y], right_ref[y]
        a_ref[y] = jnp.where(odd, left, right)
        b_ref[y] = jnp.where(odd, right, left)

    loop(rows, body)


def absorbed(optical, bound):
    series = 1 / 120
    for k in (-1 / 24, 1 / 6, -1 / 2, 1.0):
        series = series * optical + k
    series = series * optical
    return series if bound <= 0.125 else jnp.where(optical < 0.125, series, 1.0 - jnp.exp(-optical))


def march(optical, matrix, bound):
    planes = optical.shape[1]
    sums = jnp.dot(halves(optical), matrix, preferred_element_type=F32)
    transmit = jnp.exp(-sums[:, :planes])
    q = transmit * absorbed(optical, bound)
    return q, transmit - q, sums[:, planes:]


def inner_kernel(
    all_planes, d_ref, e_ref, row_taps_ref, row_shift_ref, taps_ref, shift_ref, scale_ref, cotangent_ref,
    rd_ref, re_ref, q_ref, p_ref, dense_ref, weight_ref,
):
    rows, columns, planes = d_ref.shape
    row_bits = bits_of(row_shift_ref[...])
    row_taps = rows_of(row_taps_ref[...])
    pitch = pitch_of(columns)
    per = 128 // columns
    cotangent = jnp.transpose(cotangent_ref[...])
    for group in range(rows // SUB):
        at = group % per * columns
        weight_ref[group // per, :, at : at + columns] = cotangent[group * SUB : (group + 1) * SUB, :]

    def row_body(t):
        at = pl.multiple_of(t * SUB, SUB)
        for ref, out in ((d_ref, rd_ref), (e_ref, re_ref)):
            get = lambda y: ref[y, pl.ds(at, SUB), :] if 0 <= y < rows else None
            for y, v in resample(get, row_bits, row_taps, range(rows), False):
                out[pl.ds(y * pitch + at, SUB), :] = v

    loop(columns // SUB, row_body)
    bits = bits_of(shift_ref[...])
    taps = rows_of(taps_ref[...])
    scale = jnp.broadcast_to(scale_ref[...] / all_planes, (SUB, planes))
    before, after = scan_matrix(planes, True), scan_matrix(planes, False)
    dense_ref[...] = jnp.zeros_like(dense_ref)
    inside = range(HALO, columns - HALO)

    def body(group):
        y0 = group * SUB
        at = pl.multiple_of(y0, SUB)
        get = column_get(rd_ref, None, y0, columns)
        optical = jnp.concatenate([scale * v for _, v in resample(get, bits, taps, inside, False)], axis=0)
        q, n, totals = march(optical, before, LARGEST / all_planes)
        pack_totals(totals, dense_ref.at[0], group, columns, inside)
        get = column_get(re_ref, None, y0, columns)
        emission = jnp.concatenate([v for _, v in resample(get, bits, taps, inside, False)], axis=0)
        sums = jnp.dot(halves(q * emission), after, preferred_element_type=F32)
        pack_totals(sums[:, planes:], dense_ref.at[1], group, columns, inside)
        p = n * emission - sums[:, :planes]
        for i in range(len(inside)):
            q_ref[i, pl.ds(at, SUB), :] = q[i * SUB : (i + 1) * SUB]
            p_ref[i, pl.ds(at, SUB), :] = scale * p[i * SUB : (i + 1) * SUB]

    loop(rows // SUB, body)


def row_halo(odd, a_ref, b_ref, halo_ref, bits, taps):
    rows = a_ref.shape[0]
    for side in range(2):
        use_a = odd if side == 0 else ~odd
        get = lambda y: jnp.where(use_a, a_ref[y], b_ref[y]) if 0 <= y < rows else None
        for y, v in resample(get, bits, taps, range(rows), False):
            halo_ref[pl.ds(y * pitch_of(2 * HALO) + side * HALO, SUB), :] = v


def column_get(r_ref, halo_ref, y0, columns):
    pitch, side_pitch = pitch_of(columns), pitch_of(2 * HALO)

    def get(x):
        reach = 0 if halo_ref is None else HALO
        if x < -reach or x >= columns + reach:
            return None
        if x < 0:
            return halo_ref[pl.ds(y0 * side_pitch + x + HALO, SUB, stride=side_pitch), :]
        if x >= columns:
            return halo_ref[pl.ds(y0 * side_pitch + HALO + x - columns, SUB, stride=side_pitch), :]
        return r_ref[pl.ds(y0 * pitch + x, SUB, stride=pitch), :]

    return get


def pack_totals(totals, dense_ref, group, columns, inside):
    lane = lax.broadcasted_iota(jnp.int32, (SUB, 128), 1)
    per = 128 // columns
    packed = jnp.zeros((SUB, 128), F32)
    base = (group % per) * columns
    for i, x in enumerate(inside):
        packed = jnp.where(lane == base + x, totals[i * SUB : (i + 1) * SUB, :], packed)
    dense_ref[group // per] += packed


def outside_of(columns):
    return [*range(HALO), *range(columns - HALO, columns)]


def split_edges(odd, refs, a_ref, b_ref):
    rows = refs[0].shape[1]

    def body(group):
        at = pl.ds(pl.multiple_of(group * SUB, SUB), SUB)
        for n, ref in enumerate(refs):
            for i in range(HALO):
                left, right = ref[i, at, :], ref[HALO + i, at, :]
                a_ref[n * HALO + i, at, :] = jnp.where(odd, left, right)
                b_ref[n * HALO + i, at, :] = jnp.where(odd, right, left)

    loop(rows // SUB, body)


def density_kernel(
    all_planes, odd_ref, rd_ref, b_ref, a_ref, inner_ref, row_taps_ref, row_shift_ref, taps_ref, shift_ref, scale_ref,
    q_ref, n_ref, dense_ref, halo_ref,
):
    odd = odd_ref[0] == 1
    rows, planes = q_ref.shape[1:]
    columns = rd_ref.shape[0] // rows - 1
    row_halo(odd, a_ref, b_ref, halo_ref, bits_of(row_shift_ref[...]), rows_of(row_taps_ref[...]))
    bits = bits_of(shift_ref[...])
    taps = rows_of(taps_ref[...])
    scale = jnp.broadcast_to(scale_ref[...] / all_planes, (SUB, planes))
    matrix = scan_matrix(planes, True)
    dense_ref[...] = inner_ref[0]
    outside = outside_of(columns)

    def body(group):
        y0 = group * SUB
        at = pl.multiple_of(y0, SUB)
        get = column_get(rd_ref, halo_ref, y0, columns)
        optical = jnp.concatenate([scale * v for _, v in resample(get, bits, taps, outside, False)], axis=0)
        q, n, totals = march(optical, matrix, LARGEST / all_planes)
        for i in range(len(outside)):
            q_ref[i, pl.ds(at, SUB), :] = q[i * SUB : (i + 1) * SUB]
            n_ref[i, pl.ds(at, SUB), :] = n[i * SUB : (i + 1) * SUB]
        pack_totals(totals, dense_ref, group, columns, outside)

    loop(rows // SUB, body)


def emission_kernel(
    all_planes, odd_ref, re_ref, b_ref, a_ref, q_ref, n_ref, inner_ref, optical_ref, row_taps_ref, row_shift_ref, taps_ref, shift_ref, scale_ref,
    p_ref, pa_ref, pb_ref, dense_ref, halo_ref,
):
    odd = odd_ref[0] == 1
    rows, planes = p_ref.shape[1:]
    columns = re_ref.shape[0] // rows - 1
    row_halo(odd, a_ref, b_ref, halo_ref, bits_of(row_shift_ref[...]), rows_of(row_taps_ref[...]))
    bits = bits_of(shift_ref[...])
    taps = rows_of(taps_ref[...])
    scale = jnp.broadcast_to(scale_ref[...] / all_planes, (SUB, planes))
    matrix = scan_matrix(planes, False)
    dense_ref[0] = optical_ref[...]
    dense_ref[1] = inner_ref[1]
    outside = outside_of(columns)

    def body(group):
        y0 = group * SUB
        at = pl.multiple_of(y0, SUB)
        get = column_get(re_ref, halo_ref, y0, columns)
        pieces = [v for _, v in resample(get, bits, taps, outside, False)]
        light = jnp.concatenate([q_ref[i, pl.ds(at, SUB), :] * v for i, v in enumerate(pieces)], axis=0)
        sums = jnp.dot(halves(light), matrix, preferred_element_type=F32)
        for i, v in enumerate(pieces):
            behind = sums[i * SUB : (i + 1) * SUB, :planes]
            p_ref[i, pl.ds(at, SUB), :] = scale * (n_ref[i, pl.ds(at, SUB), :] * v - behind)
        pack_totals(sums[:, planes:], dense_ref.at[1], group, columns, outside)

    loop(rows // SUB, body)
    split_edges(odd, (p_ref, q_ref), pa_ref, pb_ref)


def join_kernel(count, where_ref, weight_ref, *refs):
    sums, out_ref = refs[:count], refs[count]
    mine = where_ref[1]
    for c in range(weight_ref.shape[0]):
        front = jnp.zeros_like(weight_ref[c])
        for ahead in range(1, count):
            front += jnp.where(mine + ahead >= count, sums[ahead][0, c], 0.0)
        running = front + sums[0][0, c]
        back = jnp.zeros_like(front)
        for ahead in range(1, count):
            there = mine + ahead < count
            back += jnp.where(there, jnp.exp(-running) * sums[ahead][1, c], 0.0)
            running += jnp.where(there, sums[ahead][0, c], 0.0)
        out_ref[0, c] = weight_ref[c] * jnp.exp(-front)
        out_ref[1, c] = weight_ref[c] * back


def lay(split_ref, row, dense, base, first, count):
    lane = lax.broadcasted_iota(jnp.int32, (SUB, 128), 1)
    masks = [lane == base + first + x for x in range(count)]
    hi = dense.astype(BF16).astype(F32)
    stacks = [
        jnp.concatenate([jnp.where(m, part, 0.0) for m in masks], axis=0).astype(BF16) for part in (hi, dense - hi)
    ]
    split_ref[row : row + count * SUB, :] = jnp.concatenate(stacks, axis=1)


def spread(split_ref, out_ref):
    out_ref[...] = jnp.dot(split_ref[...], jnp.ones((256, 128), BF16), preferred_element_type=F32)


def finish_rows(ref, pitch, at, bits, taps, held, out, sems):
    rows = held.shape[0]
    half = rows // 2
    copies = []
    get = lambda y: ref[pl.ds(y * pitch + at, SUB), :] if 0 <= y < rows else None
    for y, v in resample(get, bits, taps, range(rows), True):
        held[y] = v
        if y % half == half - 1:
            part = pl.ds(y + 1 - half, half)
            copies.append(pltpu.make_async_copy(held.at[part], out.at[part], sems.at[y // half]))
            copies[-1].start()
    return copies


def own_kernel(
    all_planes, p_in, q_in, p_out, q_out, own_ref, row_taps_ref, row_shift_ref, taps_ref, shift_ref, scale_ref,
    gd_ref, ge_ref, td_ref, te_ref, cd_ref, ce_ref, held_ref, split_ref, weight_ref, sems,
):
    inner, rows, planes = p_in.shape
    columns = inner + 2 * HALO
    per = 128 // columns
    groups = rows // SUB
    pitch, side_pitch = pitch_of(inner), pitch_of(2 * HALO)
    bits = bits_of(shift_ref[...])
    taps = rows_of(taps_ref[...])
    scale = jnp.broadcast_to(scale_ref[...] / all_planes, (SUB, planes))

    for group in range(groups):
        lay(split_ref, group * columns * SUB, own_ref[0, group // per], group % per * columns, 0, columns)
    spread(split_ref, weight_ref)

    for group in range(groups):
        y0 = group * SUB
        back = own_ref[1, group // per]

        def front_at(x):
            row = (group * columns + x) * SUB
            return weight_ref[row : row + SUB, :]

        def back_at(x):
            lane = group % per * columns + x
            return jnp.broadcast_to(back[:, lane : lane + 1], (SUB, 128)) * scale

        def local(inside, outside, x):
            if HALO <= x < columns - HALO:
                return inside[x - HALO, y0 : y0 + SUB, :]
            return outside[x if x < HALO else x - inner, y0 : y0 + SUB, :]

        def get_d(x):
            if not 0 <= x < columns:
                return None
            return front_at(x) * local(p_in, p_out, x) - back_at(x)

        def get_e(x):
            if not 0 <= x < columns:
                return None
            return front_at(x) * local(q_in, q_out, x)

        for get, inside, outside in ((get_d, cd_ref, td_ref), (get_e, ce_ref, te_ref)):
            for x, v in resample(get, bits, taps, range(columns), True):
                if HALO <= x < columns - HALO:
                    inside[pl.ds(y0 * pitch + x - HALO, SUB, stride=pitch), :] = v
                else:
                    to = x if x < HALO else x - inner
                    outside[pl.ds(y0 * side_pitch + to, SUB, stride=side_pitch), :] = v

    row_bits = bits_of(row_shift_ref[...])
    row_taps = rows_of(row_taps_ref[...])
    copies = []
    for f, (ref, out) in enumerate(((cd_ref, gd_ref), (ce_ref, ge_ref))):
        for t in range(inner // SUB):
            copies += finish_rows(
                ref, pitch, t * SUB, row_bits, row_taps, held_ref.at[f, t],
                out.at[:, pl.ds(HALO + t * SUB, SUB), :], sems.at[f, t],
            )
    for c in copies:
        c.wait()


def outer_kernel(
    all_planes, odd_ref, pa_ref, pb_ref, wb_ref, wa_ref, td_ref, te_ref,
    row_taps_ref, row_shift_ref, taps_ref, shift_ref, scale_ref, gd_in, ge_in,
    gd_ref, ge_ref, cd_ref, ce_ref, held_ref, split_ref, weight_ref, sems,
):
    odd = odd_ref[0] == 1
    rows, columns, planes = gd_ref.shape
    per = 128 // columns
    groups = rows // SUB
    pitch = pitch_of(2 * HALO)
    bits = bits_of(shift_ref[...])
    taps = rows_of(taps_ref[...])
    scale = jnp.broadcast_to(scale_ref[...] / all_planes, (SUB, planes))
    use_a = (odd, ~odd)

    for side in range(2):
        for group in range(groups):
            row = (side * groups + group) * HALO * SUB
            dense = jnp.where(use_a[side], wa_ref[0, group // per], wb_ref[0, group // per])
            lay(split_ref, row, dense, group % per * columns, columns - HALO if side == 0 else 0, HALO)
    spread(split_ref, weight_ref)

    for group in range(groups):
        y0 = group * SUB
        for side in range(2):
            start = -HALO if side == 0 else HALO
            back = jnp.where(use_a[side], wa_ref[1, group // per], wb_ref[1, group // per])

            def front_at(i):
                row = ((side * groups + group) * HALO + i) * SUB
                return weight_ref[row : row + SUB, :]

            def back_at(i):
                lane = group % per * columns + i + (columns - HALO if side == 0 else 0)
                return jnp.broadcast_to(back[:, lane : lane + 1], (SUB, 128)) * scale

            def get_d(x):
                i = x - start
                if not 0 <= i < HALO:
                    return None
                v = jnp.where(use_a[side], pa_ref[i, y0 : y0 + SUB, :], pb_ref[i, y0 : y0 + SUB, :])
                return front_at(i) * v - back_at(i)

            def get_e(x):
                i = x - start
                if not 0 <= i < HALO:
                    return None
                v = jnp.where(use_a[side], pa_ref[HALO + i, y0 : y0 + SUB, :], pb_ref[HALO + i, y0 : y0 + SUB, :])
                return front_at(i) * v

            for get, ref, out in ((get_d, td_ref, cd_ref), (get_e, te_ref, ce_ref)):
                for x, v in resample(get, bits, taps, range(HALO), True):
                    at = pl.ds(y0 * pitch + side * HALO + x, SUB, stride=pitch)
                    out[at, :] = ref[at, :] if v is None else ref[at, :] + v

    row_bits = bits_of(row_shift_ref[...])
    row_taps = rows_of(row_taps_ref[...])
    copies = []
    for f, (ref, out) in enumerate(((cd_ref, gd_ref), (ce_ref, ge_ref))):
        for side in range(2):
            copies += finish_rows(
                ref, pitch, side * HALO, row_bits, row_taps, held_ref.at[f, side],
                out.at[:, pl.ds(side * (columns - HALO), HALO), :], sems.at[f, side],
            )
    for c in copies:
        c.wait()


def near(value):
    big = value.size >= 1 << 16
    return pltpu.with_memory_space_constraint(value, pltpu.VMEM) if big else value


def call(kernel, outs, scalars, vmem, scratch=(), hbm_in=(), hbm_out=0, aliases=None, micros=2.0, limit=VMEM_LIMIT):
    whole, far = pl.BlockSpec(memory_space=pltpu.VMEM), pl.BlockSpec(memory_space=pl.ANY)
    return pl.pallas_call(
        kernel,
        out_shape=[jax.ShapeDtypeStruct(s, F32) if i < hbm_out else pltpu.VMEM(s, F32) for i, s in enumerate(outs)],
        in_specs=[pl.BlockSpec(memory_space=pltpu.SMEM)] * len(scalars)
        + [whole] * len(vmem)
        + [far] * len(hbm_in),
        out_specs=[far] * hbm_out + [whole] * (len(outs) - hbm_out),
        scratch_shapes=list(scratch),
        input_output_aliases=aliases or {},
        compiler_params=pltpu.CompilerParams(vmem_limit_bytes=limit),
        cost_estimate=pl.CostEstimate(
            flops=int(micros * 1e6), bytes_accessed=int(micros * 3.0e6), transcendentals=0
        ),
    )(*scalars, *[near(v) for v in vmem], *[pltpu.with_memory_space_constraint(v, pltpu.HBM) for v in hbm_in])


def swap(value, axis, parity):
    count = lax.axis_size(axis)
    pairs = []
    for i in range(parity, count - 1, 2):
        pairs += [(i, i + 1), (i + 1, i)]
    return lax.ppermute(value, axis, pairs)


def on_device(density, emission, taps, shift, row_taps, row_shift, step_length, cotangent):
    rows, columns, planes = density.shape
    slabs = lax.axis_size("depth")
    all_planes = planes * slabs
    per = 128 // columns
    chunks = rows // SUB // per
    shift, row_shift = shift[None, :], row_shift[None, :]
    scale = step_length[None, :]
    place = jnp.stack([lax.axis_index("screen") % 2, lax.axis_index("depth")]).astype(jnp.int32)
    where = jnp.broadcast_to(place[:, None, None], (2, SUB, 128))
    edge = (rows, HALO, planes)
    sides = []
    for field in (density, emission):
        a, b = call(
            edge_kernel,
            [edge] * 2,
            [],
            [where],
            [pltpu.VMEM(edge, F32), pltpu.VMEM(edge, F32), pltpu.SemaphoreType.DMA((2,))],
            hbm_in=[field],
            micros=0.2,
        )
        sides.append((swap(a, "screen", 0), swap(b, "screen", 1)))
    (da, db), (ea, eb) = sides
    flat = (rows * pitch_of(columns), planes)
    inside = (columns - 2 * HALO, rows, planes)
    outside = (2 * HALO, rows, planes)
    side = (HALO, rows, planes)
    dense = (chunks, SUB, 128)
    rd, re, q_in, p_in, inner_sums, weight = call(
        functools.partial(inner_kernel, all_planes),
        [flat, flat, inside, inside, (2,) + dense, dense],
        [],
        [density, emission, row_taps, row_shift, taps, shift, scale, cotangent.T],
        micros=3.0,
    )
    outer = (rows * pitch_of(2 * HALO), planes)
    q_out, n_out, slab_optical = call(
        functools.partial(density_kernel, all_planes),
        [outside, outside, dense],
        [],
        [where, rd, db, da, inner_sums, row_taps, row_shift, taps, shift, scale],
        [pltpu.VMEM(outer, F32)],
    )
    p_out, pa, pb, state = call(
        functools.partial(emission_kernel, all_planes),
        [outside, outside, outside, (2,) + dense],
        [],
        [where, re, eb, ea, q_out, n_out, inner_sums, slab_optical, row_taps, row_shift, taps, shift, scale],
        [pltpu.VMEM(outer, F32)],
        micros=6.0,
    )
    pa, pb = swap(pa, "screen", 0), swap(pb, "screen", 1)
    ahead = [state] + [
        lax.ppermute(state, "depth", [((i + e) % slabs, i) for i in range(slabs)]) for e in range(1, slabs)
    ]
    (own,) = call(
        functools.partial(join_kernel, slabs), [(2,) + dense], [], [where, weight] + ahead, micros=0.1
    )
    wa, wb = swap(own, "screen", 0), swap(own, "screen", 1)
    inner = (rows * pitch_of(columns - 2 * HALO), planes)
    halves_of = rows * columns
    gd, ge, td, te = call(
        functools.partial(own_kernel, all_planes),
        [density.shape, density.shape, outer, outer],
        [],
        [p_in, q_in, p_out, q_out, own, row_taps, row_shift, taps, shift, scale],
        [
            pltpu.VMEM(inner, F32),
            pltpu.VMEM(inner, F32),
            pltpu.VMEM((2, (columns - 2 * HALO) // SUB, rows, SUB, planes), F32),
            pltpu.VMEM((halves_of, 256), BF16),
            pltpu.VMEM((halves_of, planes), F32),
            pltpu.SemaphoreType.DMA((2, (columns - 2 * HALO) // SUB, 2)),
        ],
        hbm_out=2,
        micros=6.0,
    )
    halves_of = rows * HALO * 2
    gd, ge = call(
        functools.partial(outer_kernel, all_planes),
        [density.shape, density.shape],
        [],
        [where, pa, pb, wb, wa, td, te, row_taps, row_shift, taps, shift, scale],
        [
            pltpu.VMEM(outer, F32),
            pltpu.VMEM(outer, F32),
            pltpu.VMEM((2, 2, rows, HALO, planes), F32),
            pltpu.VMEM((halves_of, 256), BF16),
            pltpu.VMEM((halves_of, planes), F32),
            pltpu.SemaphoreType.DMA((2, 2, 2)),
        ],
        hbm_in=[gd, ge],
        hbm_out=2,
        aliases={12: 0, 13: 1},
    )
    return gd, ge


def solution(mesh):
    in_specs = (
        P("groups", "screen", "depth"),
        P("groups", "screen", "depth"),
        P("groups", "depth"),
        P(("groups", "depth")),
        P("groups", "depth"),
        P(("groups", "depth")),
        P(("groups", "depth")),
        P("groups", "screen"),
    )
    out_specs = (P("groups", "screen", "depth"), P("groups", "screen", "depth"))
    return jax.shard_map(
        on_device, mesh=mesh, in_specs=in_specs, out_specs=out_specs, check_vma=False
    )
```
